256 devices in a mesh: dp: 64 (over x, z, core), rep: 4 (over y).
Axes of the slice: x: 4, y: 4, z: 8, core: 2. Of those that a mesh axis runs over, the one named last changes fastest.
Arguments:
- embeddings: bfloat16 [262144, 768], P('dp'), as said below
- valid_rows: int32 [512], replicated, may hold values from 64 to 512, as said below
- pair_table: int32 [64, 64], replicated, may hold values from -1 to 63, as said below
Outputs:
- best_similarity: float32 [262144], P('dp')
The draws below stay inside these ranges and needn't reach their ends.
Inputs may be any that keep to these rules, and one draw needn't show every extreme that they name: `embeddings`: embeddings are finite; rows need no particular norm. Block k holds valid_rows[k] valid rows, which come first in the block. `pair_table`: entry [a, b] is -1 or i * 8 + j, naming block i of device a and block j of device b; at most one of [a, b] and [b, a] is not -1, and the diagonal is -1.
All inputs are finite; a program needn't handle non-finite values.
Results may differ from the reference program's by a relative error of at most 0.00036.
Values may be sent and summed in bfloat16 or wider, within the bound.
No kernel may reach another device: no remote copies, remote signals or barrier semaphores. Data moves between devices by JAX's collectives and lax.ppermute only.
A program may use at most 128 MiB of HBM per device.

```python
import math
import jax
import jax.numpy as jnp
from jax import lax

D = 768
BLOCK = 512
BLK_DEV = 8
BLOCKS = 512
ROWS = 262144
N_DP = 64


def pair_layout(key):
    key = jax.random.fold_in(key, 37)
    key_weight, key_exists, key_code = jax.random.split(key, 3)
    weight = jax.random.randint(key_weight, (N_DP,), 0, 8)
    exists = jax.random.randint(key_exists, (N_DP, N_DP), 0, 20) < 17
    pair_code = jax.random.randint(key_code, (N_DP, N_DP), 0, BLK_DEV * BLK_DEV)
    device_ids = jnp.arange(N_DP, dtype=jnp.int32)
    upper = device_ids[:, None] < device_ids[None, :]
    forced = (device_ids[:, None] == 0) & (device_ids[None, :] == 1)
    exists = exists & upper | forced
    pair_code = jnp.where(forced, BLK_DEV * BLK_DEV - 1, pair_code)
    to_row = weight[:, None] >= weight[None, :]
    keep_upper = exists & to_row
    keep_lower = (exists & jnp.logical_not(to_row)).T
    swapped = (pair_code % BLK_DEV * BLK_DEV + pair_code // BLK_DEV).T
    table = jnp.where(keep_upper, pair_code, jnp.where(keep_lower, swapped, -1))
    return table.astype(jnp.int32)


def block_partners(table):
    codes = table.reshape(-1)
    entry_ids = jnp.arange(N_DP * N_DP, dtype=jnp.int32)
    live = codes >= 0
    first = jnp.where(live, entry_ids // N_DP * BLK_DEV + codes // BLK_DEV, BLOCKS)
    second = jnp.where(live, entry_ids % N_DP * BLK_DEV + codes % BLK_DEV, BLOCKS)
    partner = jnp.full((BLOCKS,), -1, jnp.int32)
    partner = partner.at[first].max(jnp.where(live, second, -1), mode='drop')
    partner = partner.at[second].max(jnp.where(live, first, -1), mode='drop')
    return partner


def draw_embeddings(key, part):
    table = pair_layout(key)
    key = jax.random.fold_in(key, 11)
    keys = jax.random.split(key, 8)
    partner = block_partners(table)
    row_ids = jnp.arange(ROWS, dtype=jnp.int32)
    row_block = row_ids // BLOCK
    kind = jax.random.randint(keys[0], (ROWS,), 0, 20)
    block_partner = jnp.take(partner, row_block)
    use_pair = (kind < 4) & (block_partner >= 0)
    use_local = (kind >= 4) & (kind < 6)
    device_block = row_block // BLK_DEV * BLK_DEV + jax.random.randint(keys[1], (ROWS,), 0, BLK_DEV)
    source_block = jnp.where(use_pair, block_partner, device_block)
    source_row = source_block * BLOCK + jax.random.randint(keys[2], (ROWS,), 0, max(BLOCK // 8, 1))
    copied = use_pair | use_local
    row_scale = jnp.exp(jax.random.uniform(keys[3], (ROWS, 1), jnp.float32, 0.0, math.log(10.0)))
    common = jax.random.normal(keys[4], (1, D), jnp.float32)
    spread_noise = jax.random.uniform(keys[5], (ROWS, 1), jnp.float32, 0.1, 0.5)
    jitter = jax.random.normal(keys[6], (ROWS, D), jnp.float32)
    fresh = jax.random.normal(keys[7], (ROWS, D), jnp.float32)
    values = jitter + 0.1 * common
    copies = jnp.take(values, source_row, axis=0) + spread_noise * fresh
    values = jnp.where(copied[:, None], copies, values)
    return (row_scale * values).astype(jnp.bfloat16)


def draw_valid_rows(key, part):
    key = jax.random.fold_in(key, 23)
    drawn = jax.random.randint(key, (BLOCKS,), BLOCK // 8, BLOCK + BLOCK // 3 + 1)
    counts = jnp.minimum(drawn, BLOCK)
    return counts.at[0].set(BLOCK).astype(jnp.int32)


def draw_pair_table(key, part):
    table = pair_layout(key)
    return table


def setup_inputs(seed: int = 0) -> dict:
    key_of = jax.random.split(jax.random.key(seed), 4)
    embeddings = draw_embeddings(jax.random.fold_in(key_of[3], 71), 0)
    valid_rows = draw_valid_rows(jax.random.fold_in(key_of[3], 71), 0)
    pair_table = draw_pair_table(jax.random.fold_in(key_of[3], 71), 0)
    return {"embeddings": embeddings, "valid_rows": valid_rows, "pair_table": pair_table}


absent = -2.0
epsilon = 1e-06

def compare(left, right):
    return jnp.dot(left.astype(jnp.float32), right.astype(jnp.float32).T, preferred_element_type=jnp.float32)

def reference(embeddings, valid_rows, pair_table):
    as_float = embeddings.astype(jnp.float32)
    unit_rows = (as_float * lax.rsqrt(lax.optimization_barrier(jnp.sum(as_float * as_float, axis=1, keepdims=True)) + epsilon)).astype(jnp.bfloat16)
    unit_blocks = unit_rows.reshape(BLOCKS, BLOCK, D)
    positions = jnp.arange(BLOCK, dtype=jnp.int32)
    valid = positions[None, :] < valid_rows[:, None]
    device_rows = unit_rows.reshape(N_DP, BLK_DEV * BLOCK, D)
    device_valid = valid.reshape(N_DP, BLK_DEV * BLOCK)
    column_ids = jnp.arange(BLK_DEV * BLOCK, dtype=jnp.int32)

    def local(pieces):
        rows_all, rows_ok = pieces

        def one_block(block_index):
            rows_here = lax.dynamic_slice_in_dim(rows_all, block_index * BLOCK, BLOCK, 0)
            scores = compare(rows_here, rows_all)
            row_ids = block_index * BLOCK + positions
            allowed = rows_ok[None, :] & (row_ids[:, None] != column_ids[None, :])
            return lax.optimization_barrier(jnp.max(jnp.where(allowed, scores, absent), axis=1))
        return lax.map(one_block, jnp.arange(BLK_DEV, dtype=jnp.int32))
    best_score = lax.map(local, (device_rows, device_valid)).reshape(BLOCKS, BLOCK)
    entries = pair_table.reshape(-1)
    entry_ids = jnp.arange(N_DP * N_DP, dtype=jnp.int32)

    def visit(running, pieces):
        pair_code, entry_id = pieces
        first_block = entry_id // N_DP * BLK_DEV + pair_code // BLK_DEV
        second_block = entry_id % N_DP * BLK_DEV + pair_code % BLK_DEV

        def compare_pair(current):
            first_rows = lax.dynamic_index_in_dim(unit_blocks, first_block, 0, keepdims=False)
            second_rows = lax.dynamic_index_in_dim(unit_blocks, second_block, 0, keepdims=False)
            first_ok = lax.dynamic_index_in_dim(valid, first_block, 0, keepdims=False)
            second_ok = lax.dynamic_index_in_dim(valid, second_block, 0, keepdims=False)
            scores = compare(first_rows, second_rows)
            row_max = lax.optimization_barrier(jnp.max(jnp.where(second_ok[None, :], scores, absent), axis=1))
            col_max = lax.optimization_barrier(jnp.max(jnp.where(first_ok[:, None], scores, absent), axis=0))
            current = current.at[first_block].max(row_max)
            return current.at[second_block].max(col_max)
        return (lax.cond(pair_code >= 0, compare_pair, lambda current: current, running), None)
    best_score, _ = lax.scan(visit, best_score, (entries, entry_ids))
    return jnp.where(valid, best_score, -1.0).reshape(-1)
```

```python
import functools

import jax
import jax.numpy as jnp
from jax import lax
from jax.experimental import pallas as pl
from jax.experimental.pallas import tpu as pltpu
from jax.sharding import Mesh, PartitionSpec as P

absent = -2.0
epsilon = 1e-06
n_x, n_z, n_core, n_rep = 4, 8, 2, 4
chips = n_x * n_z
blocks = 8
rows = 512
quarter = rows // n_rep
width = 768
vmem_bytes = 60 << 20


def dot_t(left, right):
    return lax.dot_general(
        left, right, (((1,), (1,)), ((), ())), preferred_element_type=jnp.float32
    )


def normalise(raw):
    wide = raw.astype(jnp.float32)
    scale = lax.rsqrt(jnp.sum(wide * wide, axis=-1, keepdims=True) + epsilon)
    return (wide * scale).astype(jnp.bfloat16)


def place():
    return lax.axis_index("x"), lax.axis_index("z"), lax.axis_index("core"), lax.axis_index("rep")


def pair_info(table, source, target, core, many, which):
    side = which if many == 2 else jnp.where(source < target, core, 1 - core)
    forth = table[source * n_core + core, target * n_core + side]
    back = table[target * n_core + side, source * n_core + core]
    live = (forth >= 0) | (back >= 0)
    if many == 1:
        live = live & ((source != target) | (core == 0))
    source_block = jnp.where(forth >= 0, forth >> 3, back & 7)
    target_block = jnp.where(forth >= 0, forth & 7, (back >> 3) & 7)
    return live, side, source_block, target_block


def chip_at(x, z, dx, dz):
    return ((x + dx + n_x) & (n_x - 1)) * n_z + ((z + dz + n_z) & (n_z - 1))


first = [[(dx, 0, 1, 0), (dx, 1, 2, 0), (dx, 1, 2, 1)] for dx in range(n_x)]
second = [[(dx, 2, 2, 0), (dx, 2, 2, 1)] for dx in range(n_x)]
third = [[(dx, 3, 2, 0), (dx, 3, 2, 1)] for dx in range(n_x)]
far = [(dx, 4, 1, 0) for dx in range(n_x)]
stage_a = sum(first, [])
stage_b = sum(third + second, []) + far


def prep_kernel(table, emb, units, to0, to1, to2, to3, raw, unit, sem_in, sems):
    x, z, core, rep = place()
    load = pltpu.make_async_copy(emb.at[:, pl.ds(rep * quarter, quarter), :], raw, sem_in)
    load.start()
    load.wait()

    def one(b, carry):
        unit[b] = normalise(raw[b])
        return carry

    lax.fori_loop(0, blocks, one, 0)
    copies = [pltpu.make_async_copy(unit, units, sem_in)]
    copies[0].start()
    for dx, out in enumerate((to0, to1, to2, to3)):
        _, _, block, _ = pair_info(table, chip_at(x, z, 0, 0), chip_at(x, z, dx, 4), core, 1, 0)
        copies.append(pltpu.make_async_copy(unit.at[block], out.at[0], sems.at[dx]))
        copies[-1].start()
    for copy in copies:
        copy.wait()


def pick_kernel(wanted, sources, spread, table, *refs):
    held = dict(zip(sources, refs))
    parts, get_sems, put_sems = refs[-3:]
    x, z, core, rep = place()
    n = len(wanted)
    if spread:
        last = refs[-4]
        outs = list(refs[-n + n_x - 4 : -4]) + [last.at[(x + dx) & (n_x - 1)] for dx in range(n_x)]
    else:
        outs = refs[-n - 3 : -3]
    gone_of = max(sources)
    gets, puts = [], []
    for a, slots in enumerate(wanted):
        for place_in, (dx, dz, many, which) in enumerate(slots):
            gone = 0 if dz == 0 else gone_of
            source, target = chip_at(x, z, 0, -gone), chip_at(x, z, dx, dz - gone)
            _, _, block, _ = pair_info(table, source, target, core, many, which)
            come = held[gone].at[block]
            gets.append(
                pltpu.make_async_copy(come, parts.at[a, place_in], get_sems.at[3 * a + place_in])
            )
            gets[-1].start()
    left = list(gets)
    for a, (out, slots) in enumerate(zip(outs, wanted)):
        for _ in slots:
            left.pop(0).wait()
        puts.append(
            pltpu.make_async_copy(parts.at[a, pl.ds(0, len(slots))], out, put_sems.at[a])
        )
        puts[-1].start()
    for copy in puts:
        copy.wait()


def local_kernel(valid, own, sib, cols, unit_out, best):
    step = pl.program_id(0)
    x, z, core, rep = place()
    dev = chip_at(x, z, 0, 0) * n_core + core
    start = rep * quarter

    @pl.when(step >= blocks)
    def _():
        unit_out[0] = normalise(sib[0])

    @pl.when(step < blocks)
    def _():
        mine = normalise(own[0])
        unit_out[0] = mine
        part = lax.broadcasted_iota(jnp.int32, (quarter, rows), 0)
        gap = lax.broadcasted_iota(jnp.int32, (quarter, rows), 1) - part
        found = jnp.full((1, rows), absent, jnp.float32)
        for k in range(0, blocks, 2):
            pair = jnp.concatenate([cols[k], cols[k + 1]], axis=0)
            scores = dot_t(pair, mine)
            for half in range(2):
                count = valid[dev * blocks + k + half] - start
                own_gap = jnp.where(k + half == step, start, rows)
                allowed = (part < count) & (gap != own_gap)
                here = jnp.where(allowed, scores[half * quarter : (half + 1) * quarter], absent)
                found = jnp.maximum(found, jnp.max(here, axis=0, keepdims=True))
        best[pl.ds(step, 1), :] = found


def pair_kernel(stage, feeds, before, table, valid, own, *refs):
    past, refs = refs[: 2 * len(before)], refs[2 * len(before) :]
    arrays, scratch = refs, refs[-8:]
    units, held, cols, many, listed, owner, sem_u, sem_g = scratch
    outs = refs[-10:-8] if not before else refs[-11:-8]
    slots = len(stage)
    x, z, core, rep = place()
    chip = chip_at(x, z, 0, 0)
    start = rep * quarter
    gets = []
    for a, (array, dx, count, base) in enumerate(feeds):
        came = arrays[array] if dx is None else arrays[array].at[(x - dx + n_x) & (n_x - 1)]
        gets.append(pltpu.make_async_copy(came, held.at[pl.ds(base, count)], sem_g.at[a]))
        gets[-1].start()
    row_out = outs[0]
    row_out[...] = jnp.full((2 * blocks, rows), absent, jnp.float32)
    for ref in past[::2]:
        row_out[...] = jnp.maximum(row_out[...], ref[...])
    cols[...] = jnp.full(cols.shape, absent, jnp.float32)
    for o in range(2 * blocks):
        many[o] = 0
    for slot, (dx, dz, m, which) in enumerate(stage):
        source = chip_at(x, z, -dx, -dz)
        live, side, source_block, target_block = pair_info(table, source, chip, core, m, which)
        mine = jnp.where(side == core, 0, blocks) + target_block
        filled = many[mine]
        listed[mine, filled] = jnp.where(live, slot, slots)
        listed[mine, filled + 1] = slots
        many[mine] = filled + live.astype(jnp.int32)
        owner[slot] = valid[(source * n_core + core) * blocks + source_block] - start
    owner[slots] = 0
    loads = []
    for o in range(2 * blocks):
        loads.append(pltpu.make_async_copy(own.at[o], units.at[o], sem_u.at[o]))

        @pl.when(many[o] > 0)
        def _():
            loads[o].start()

    part = lax.broadcasted_iota(jnp.int32, (quarter, rows), 0)
    lane = lax.broadcasted_iota(jnp.int32, (2 * quarter, rows), 1)
    for copy in gets:
        copy.wait()
    for o in range(2 * blocks):
        own_dev = chip * n_core + (core if o < blocks else 1 - core)
        own_count = valid[own_dev * blocks + o % blocks]

        @pl.when(many[o] > 0)
        def _():
            loads[o].wait()

        def visit(turn, carry):
            pair = [listed[o, 2 * turn], listed[o, 2 * turn + 1]]
            here_slot = [pair[0], jnp.minimum(pair[1], slots - 1)]
            scores = dot_t(
                jnp.concatenate([held[here_slot[0]], held[here_slot[1]]], axis=0), units[o]
            )
            ok = jnp.where(lane < own_count, scores, absent)
            folded = jnp.maximum(
                jnp.maximum(ok[:, 0:128], ok[:, 128:256]), jnp.maximum(ok[:, 256:384], ok[:, 384:512])
            )
            top = row_out[o : o + 1, :]
            for half in range(2):
                span = slice(half * quarter, (half + 1) * quarter)
                here = jnp.where(part < owner[pair[half]], scores[span], absent)
                top = jnp.maximum(top, jnp.max(here, axis=0, keepdims=True))
                cols[pl.ds(pair[half], 1), :] = jnp.max(folded[span].T, axis=0, keepdims=True)
            row_out[o : o + 1, :] = top
            return carry

        lax.fori_loop(0, (many[o] + 1) >> 1, visit, 0)
    col_out = outs[1]
    if not before:
        col_out[...] = cols[0:slots]
    else:
        outs[2][...] = row_out[blocks:]
        col_out[...] = jnp.full(col_out.shape, absent, jnp.float32)
        for done, ref in zip(before + [stage], list(past[1::2]) + [cols]):
            for slot, (dx, dz, _, which) in enumerate(done):
                col_out[pl.ds(2 * chip_at(x, z, -dx, -dz) + which, 1), :] = ref[slot : slot + 1, :]


def spread_in(running, best, rep):
    wide = jnp.concatenate([best] * n_rep, axis=1)
    lane = lax.broadcasted_iota(jnp.int32, (blocks, rows), 1)
    mine = (lane >= rep * quarter) & (lane < (rep + 1) * quarter)
    return jnp.where(mine, jnp.maximum(running, wide), running)


def merge_kernel(table, local, row_best, sib_rows, back, out, best):
    x, z, core, rep = place()
    best[...] = jnp.full((blocks, quarter), absent, jnp.float32)
    for dx, dz, many, which in stage_a + stage_b:
        target = chip_at(x, z, dx, dz)
        _, _, block, _ = pair_info(table, chip_at(x, z, 0, 0), target, core, many, which)
        best[pl.ds(block, 1), :] = jnp.maximum(
            best[pl.ds(block, 1), :], back[pl.ds(2 * target + which, 1), :]
        )
    merged = jnp.maximum(jnp.maximum(local[...], row_best[0:blocks]), sib_rows[...])
    mine = spread_in(merged, best[...], rep)
    for y in range(n_rep):
        out[y] = mine


def finish_kernel(valid, got, out):
    x, z, core, _ = place()
    dev = chip_at(x, z, 0, 0) * n_core + core
    best = jnp.max(got[...], axis=0)
    lane = lax.broadcasted_iota(jnp.int32, (1, quarter), 1)
    for b in range(blocks):
        count = valid[dev * blocks + b]
        for q in range(n_rep):
            span = best[b : b + 1, q * quarter : (q + 1) * quarter]
            out[n_rep * b + q : n_rep * b + q + 1, :] = jnp.where(
                lane + q * quarter < count, span, -1.0
            )


def move(value, dx, dz):
    if dx % n_x == 0 and dz % n_z == 0:
        return value
    steps = [
        (x * n_z + z, (x + dx) % n_x * n_z + (z + dz) % n_z) for x in range(n_x) for z in range(n_z)
    ]
    return lax.ppermute(value, ("x", "z"), steps)


def on_device(embeddings, valid_rows, pair_table):
    smem = pl.BlockSpec(memory_space=pltpu.SMEM)
    vmem = pl.BlockSpec(memory_space=pltpu.VMEM)
    hbm = pl.BlockSpec(memory_space=pl.ANY)
    params = pltpu.CompilerParams(vmem_limit_bytes=vmem_bytes)
    cost = pl.CostEstimate(flops=0, bytes_accessed=1 << 16, transcendentals=0)
    f32, bf16 = jnp.float32, jnp.bfloat16
    part = (quarter, width)
    raw = embeddings.reshape(blocks, rows, width)

    def pick(wanted, sources, spread, held, after, name):
        n = len(wanted)
        shapes = [(len(slots),) + part for slots in wanted]
        if spread:
            shapes = shapes[:-n_x] + [(n_x,) + shapes[-1]]
        return pl.pallas_call(
            functools.partial(pick_kernel, wanted, sources, spread),
            out_shape=[jax.ShapeDtypeStruct(shape, bf16) for shape in shapes],
            in_specs=[smem] + [hbm] * len(held + after),
            out_specs=[hbm] * len(shapes),
            scratch_shapes=[
                pltpu.VMEM((n, 3) + part, bf16),
                pltpu.SemaphoreType.DMA((3 * n,)),
                pltpu.SemaphoreType.DMA((n,)),
            ],
            compiler_params=params,
            cost_estimate=cost,
            name=name,
        )(pair_table, *held, *after)

    def compare(stage, feeds, arrays, before, past, after, name):
        slots = len(stage)
        shapes = [(2 * blocks, rows), (slots, quarter)]
        if before:
            shapes = [(2 * blocks, rows), (2 * chips, quarter), (blocks, rows)]
        return pl.pallas_call(
            functools.partial(pair_kernel, stage, feeds, before),
            out_shape=[jax.ShapeDtypeStruct(shape, f32) for shape in shapes],
            in_specs=[smem, smem, hbm] + [vmem] * len(past) + [hbm] * len(arrays + after),
            out_specs=[vmem] * len(shapes),
            scratch_shapes=[
                pltpu.VMEM((2 * blocks, rows, width), bf16),
                pltpu.VMEM((slots,) + part, bf16),
                pltpu.VMEM((slots // 8 * 8 + 8, quarter), f32),
                pltpu.SMEM((2 * blocks,), jnp.int32),
                pltpu.SMEM((2 * blocks, slots + 2), jnp.int32),
                pltpu.SMEM((slots + 1,), jnp.int32),
                pltpu.SemaphoreType.DMA((2 * blocks,)),
                pltpu.SemaphoreType.DMA((len(feeds),)),
            ],
            compiler_params=params,
            cost_estimate=cost,
            name=name,
        )(pair_table, valid_rows, units, *past, *arrays, *after)

    cols, *away = pl.pallas_call(
        prep_kernel,
        out_shape=[
            jax.ShapeDtypeStruct((blocks,) + part, bf16),
        ]
        + [jax.ShapeDtypeStruct((1,) + part, bf16)] * n_x,
        in_specs=[smem, hbm],
        out_specs=[hbm] * (1 + n_x),
        scratch_shapes=[
            pltpu.VMEM((blocks,) + part, bf16),
            pltpu.VMEM((blocks,) + part, bf16),
            pltpu.SemaphoreType.DMA,
            pltpu.SemaphoreType.DMA((n_x,)),
        ],
        compiler_params=params,
        cost_estimate=cost,
        name="prep",
    )(pair_table, raw)
    swap = [(0, 1), (1, 0)]
    sib_raw = lax.ppermute(raw, "core", swap)
    hop1 = move(cols, 0, 1)
    away = jnp.concatenate([move(a, dx, 0) for dx, a in enumerate(away)], axis=0)
    units, local_best = pl.pallas_call(
        local_kernel,
        grid=(2 * blocks,),
        out_shape=(
            jax.ShapeDtypeStruct((2 * blocks, rows, width), bf16),
            jax.ShapeDtypeStruct((blocks, rows), f32),
        ),
        in_specs=[
            smem,
            pl.BlockSpec((1, rows, width), lambda i: (jnp.minimum(i, blocks - 1), 0, 0)),
            pl.BlockSpec((1, rows, width), lambda i: (jnp.maximum(i - blocks, 0), 0, 0)),
            pl.BlockSpec((blocks,) + part, lambda i: (0, 0, 0)),
        ],
        out_specs=(
            pl.BlockSpec((1, rows, width), lambda i: (i, 0, 0)),
            pl.BlockSpec((blocks, rows), lambda i: (0, 0)),
        ),
        compiler_params=params,
        cost_estimate=cost,
        name="local",
    )(valid_rows, raw, sib_raw, cols)
    hop1, away, local_best = lax.optimization_barrier((hop1, away, local_best))
    hop2 = move(hop1, 0, 1)
    away = move(away, 0, -2)
    picked = pick(first, (0, 1), False, [cols, hop1], [], "pick_a")
    first_in = [move(a, dx, 0) for dx, a in enumerate(picked)]
    hop2, away = lax.optimization_barrier((hop2, away))
    picked = pick(third + second, (2,), True, [hop2], first_in, "pick_b")
    away = move(away, 0, -2)
    third_in = [move(a, dx, 1) for dx, a in enumerate(picked[:n_x])]
    second_in = lax.all_to_all(picked[n_x], "x", split_axis=0, concat_axis=0, tiled=True)

    past_a = compare(
        stage_a,
        [(dx, None, 3, 3 * dx) for dx in range(n_x)],
        first_in,
        [],
        [],
        [picked[0]],
        "pairs_a",
    )
    row_best, col_best, sib_best = compare(
        stage_b,
        [(dx, None, 2, 2 * dx) for dx in range(n_x)]
        + [(n_x, dx, 2, 2 * n_x + 2 * dx) for dx in range(n_x)]
        + [(n_x + 1, None, n_x, 4 * n_x)],
        third_in + [second_in, away],
        [stage_a],
        past_a,
        [],
        "pairs_b",
    )
    sib_rows = lax.ppermute(sib_best, "core", swap)
    back = lax.all_to_all(col_best, ("x", "z"), split_axis=0, concat_axis=0, tiled=True)
    shared = pl.pallas_call(
        merge_kernel,
        out_shape=jax.ShapeDtypeStruct((n_rep, blocks, rows), f32),
        in_specs=[smem, vmem, vmem, vmem, vmem],
        out_specs=vmem,
        scratch_shapes=[pltpu.VMEM((blocks, quarter), f32)],
        cost_estimate=cost,
        name="merge",
    )(pair_table, local_best, row_best, sib_rows, back)
    shared = lax.all_to_all(shared, "rep", split_axis=0, concat_axis=0, tiled=True)
    result = pl.pallas_call(
        finish_kernel,
        out_shape=jax.ShapeDtypeStruct((blocks * n_rep, quarter), f32),
        in_specs=[smem, vmem],
        out_specs=vmem,
        cost_estimate=cost,
        name="finish",
    )(valid_rows, shared)
    return result.reshape(-1)


def solution(mesh):
    grid = Mesh(mesh.devices.reshape(n_x, n_z, n_core, n_rep), ("x", "z", "core", "rep"))
    return jax.shard_map(
        on_device,
        mesh=grid,
        in_specs=(P(("x", "z", "core"), None), P(), P()),
        out_specs=P(("x", "z", "core")),
        check_vma=False,
    )
```

```python
import functools

import jax
import jax.numpy as jnp
from jax import lax
from jax.experimental import pallas as pl
from jax.experimental.pallas import tpu as pltpu
from jax.sharding import Mesh, PartitionSpec as P

absent = -2.0
epsilon = 1e-06
n_x, n_z, n_core, n_rep = 4, 8, 2, 4
chips = n_x * n_z
blocks = 8
rows = 512
quarter = rows // n_rep
width = 768
vmem_bytes = 60 << 20


def dot_t(left, right):
    return lax.dot_general(
        left, right, (((1,), (1,)), ((), ())), preferred_element_type=jnp.float32
    )


def normalise(raw):
    wide = raw.astype(jnp.float32)
    scale = lax.rsqrt(jnp.sum(wide * wide, axis=-1, keepdims=True) + epsilon)
    return (wide * scale).astype(jnp.bfloat16)


def place():
    return lax.axis_index("x"), lax.axis_index("z"), lax.axis_index("core"), lax.axis_index("rep")


def pair_info(table, source, target, core, many, which):
    side = which if many == 2 else jnp.where(source < target, core, 1 - core)
    forth = table[source * n_core + core, target * n_core + side]
    back = table[target * n_core + side, source * n_core + core]
    live = (forth >= 0) | (back >= 0)
    if many == 1:
        live = live & ((source != target) | (core == 0))
    source_block = jnp.where(forth >= 0, forth >> 3, back & 7)
    target_block = jnp.where(forth >= 0, forth & 7, (back >> 3) & 7)
    return live, side, source_block, target_block


def chip_at(x, z, dx, dz):
    return ((x + dx + n_x) & (n_x - 1)) * n_z + ((z + dz + n_z) & (n_z - 1))


first = [[(dx, 0, 1, 0), (dx, 1, 2, 0), (dx, 1, 2, 1)] for dx in range(n_x)]
second = [[(dx, 2, 2, 0), (dx, 2, 2, 1)] for dx in range(n_x)]
third = [[(dx, 3, 2, 0), (dx, 3, 2, 1)] for dx in (0, 1, 3)]
far = [(dx, 4, 1, 0) for dx in range(n_x)]
down = [(2, 5, 2, 0), (2, 5, 2, 1)]
stages = [sum(first, []) + far, third[0] + third[1], third[2] + down + sum(second, [])]
every = sum(stages, [])
gone_of = {0: 0, 1: 1, 2: 2, 3: 2}
at_pick, at_back, at_back_row, at_row, at_own = 0, 32, 64, 96, 128
at_stage, plan_size = [], 144
for stage in stages:
    at_stage.append(plan_size)
    plan_size += 16 + len(stage) + 1 + 16 * (len(stage) + 2)


def plan_kernel(table, valid, after, plan):
    x, z, core, rep = place()
    chip = chip_at(x, z, 0, 0)
    start = rep * quarter
    for o in range(2 * blocks):
        owner = chip * n_core + (core if o < blocks else 1 - core)
        plan[at_own + o] = valid[owner * blocks + o % blocks]
    number = 0
    for stage, base in zip(stages, at_stage):
        slots = len(stage)
        counts, lists = base + 2 * blocks, base + 2 * blocks + slots + 1
        for o in range(2 * blocks):
            plan[base + o] = 0
        for slot, (dx, dz, many, which) in enumerate(stage):
            target = chip_at(x, z, dx, dz)
            _, _, block, _ = pair_info(table, chip, target, core, many, which)
            plan[at_back + number] = block
            plan[at_back_row + number] = 2 * target + which
            if dz in gone_of:
                gone = gone_of[dz]
                source, target = chip_at(x, z, 0, -gone), chip_at(x, z, dx, dz - gone)
                _, _, block, _ = pair_info(table, source, target, core, many, which)
                plan[at_pick + number] = block
            source = chip_at(x, z, -dx, -dz)
            live, side, block, own_block = pair_info(table, source, chip, core, many, which)
            mine = jnp.where(side == core, 0, blocks) + own_block
            filled = plan[base + mine]
            plan[lists + mine * (slots + 2) + filled] = jnp.where(live, slot, slots)
            plan[lists + mine * (slots + 2) + filled + 1] = slots
            plan[base + mine] = filled + live.astype(jnp.int32)
            plan[counts + slot] = valid[(source * n_core + core) * blocks + block] - start
            plan[at_row + number] = 2 * source + which
            number += 1
        plan[counts + slots] = 0


def prep_kernel(table, emb, units, to0, to1, to2, to3, around, raw, unit, sem_in, sems):
    x, z, core, rep = place()
    chip = chip_at(x, z, 0, 0)
    loads = [
        pltpu.make_async_copy(emb.at[b, pl.ds(rep * quarter, quarter)], raw.at[b], sem_in.at[b])
        for b in range(blocks)
    ]
    for load in loads:
        load.start()
    copies = []
    for b in range(blocks):
        loads[b].wait()
        unit[b] = normalise(raw[b])
        copies.append(pltpu.make_async_copy(unit.at[b], units.at[b], sem_in.at[b]))
        copies[-1].start()
    outs = [to0.at[0], to1.at[0], to2.at[0], to3.at[0], around.at[0], around.at[1]]
    for a, (dx, dz, many, which) in enumerate(far + down):
        _, _, block, _ = pair_info(table, chip, chip_at(x, z, dx, dz), core, many, which)
        copies.append(pltpu.make_async_copy(unit.at[block], outs[a], sems.at[a]))
        copies[-1].start()
    for copy in copies:
        copy.wait()


def pick_kernel(wanted, spread, plan, *refs):
    near_by, hop = refs[:2]
    parts, get_sems, put_sems = refs[-3:]
    x, z, core, rep = place()
    n = len(wanted)
    if spread:
        outs = list(refs[-n + n_x - 4 : -4])
        outs += [refs[-4].at[(x + dx) & (n_x - 1)] for dx in range(n_x)]
    else:
        outs = refs[-n - 3 : -3]
    gets, puts = [], []
    for a, numbers in enumerate(wanted):
        for place_in, number in enumerate(numbers):
            held = near_by if every[number][1] == 0 else hop
            gets.append(
                pltpu.make_async_copy(
                    held.at[plan[at_pick + number]],
                    parts.at[a, place_in],
                    get_sems.at[3 * a + place_in],
                )
            )
            gets[-1].start()
    left = list(gets)
    for a, (out, numbers) in enumerate(zip(outs, wanted)):
        for _ in numbers:
            left.pop(0).wait()
        puts.append(
            pltpu.make_async_copy(parts.at[a, pl.ds(0, len(numbers))], out, put_sems.at[a])
        )
        puts[-1].start()
    for copy in puts:
        copy.wait()


def local_kernel(valid, own, sib, cols, unit_out, best):
    step = pl.program_id(0)
    x, z, core, rep = place()
    dev = chip_at(x, z, 0, 0) * n_core + core
    start = rep * quarter

    @pl.when(step >= blocks)
    def _():
        unit_out[0] = normalise(sib[0])

    @pl.when(step < blocks)
    def _():
        mine = normalise(own[0])
        unit_out[0] = mine
        part = lax.broadcasted_iota(jnp.int32, (quarter, rows), 0)
        gap = lax.broadcasted_iota(jnp.int32, (quarter, rows), 1) - part
        found = jnp.full((1, rows), absent, jnp.float32)
        for k in range(0, blocks, 2):
            pair = jnp.concatenate([cols[k], cols[k + 1]], axis=0)
            scores = dot_t(pair, mine)
            for half in range(2):
                count = valid[dev * blocks + k + half] - start
                own_gap = jnp.where(k + half == step, start, rows)
                allowed = (part < count) & (gap != own_gap)
                here = jnp.where(allowed, scores[half * quarter : (half + 1) * quarter], absent)
                found = jnp.maximum(found, jnp.max(here, axis=0, keepdims=True))
        best[pl.ds(step, 1), :] = found


def pair_kernel(stage, feeds, plan, own, *refs):
    final = stage == len(stages) - 1
    slots, base = len(stages[stage]), at_stage[stage]
    counts, lists = base + 2 * blocks, base + 2 * blocks + slots + 1
    units, held, cols, sem_u, sem_g = refs[-5:]
    outs, arrays, past = refs[-8 if final else -7 : -5], refs, ()
    if final:
        past, arrays = refs[: 2 * stage], refs[2 * stage :]
    x, z, core, rep = place()
    gets = []
    for a, (array, dx, count, first_slot) in enumerate(feeds):
        came = arrays[array] if dx is None else arrays[array].at[(x - dx + n_x) & (n_x - 1)]
        gets.append(pltpu.make_async_copy(came, held.at[pl.ds(first_slot, count)], sem_g.at[a]))
        gets[-1].start()
    loads = []
    for o in range(2 * blocks):
        loads.append(pltpu.make_async_copy(own.at[o], units.at[o], sem_u.at[o]))

        @pl.when(plan[base + o] > 0)
        def _():
            loads[o].start()

    row_out, col_out = outs[:2]
    row_out[...] = jnp.full((2 * blocks, rows), absent, jnp.float32)
    for ref in past[::2]:
        row_out[...] = jnp.maximum(row_out[...], ref[...])
    cols[...] = jnp.full(cols.shape, absent, jnp.float32)
    if final:
        col_out[...] = jnp.full(col_out.shape, absent, jnp.float32)
        number = 0
        for ref, done in zip(past[1::2], stages):
            for slot in range(len(done)):
                col_out[pl.ds(plan[at_row + number], 1), :] = ref[slot : slot + 1, :]
                number += 1
    part = lax.broadcasted_iota(jnp.int32, (quarter, rows), 0)
    lane = lax.broadcasted_iota(jnp.int32, (2 * quarter, rows), 1)
    for copy in gets:
        copy.wait()
    for o in range(2 * blocks):
        own_count = plan[at_own + o]

        @pl.when(plan[base + o] > 0)
        def _():
            loads[o].wait()

        def visit(turn, carry):
            at = lists + o * (slots + 2) + 2 * turn
            pair = [plan[at], plan[at + 1]]
            here_slot = [pair[0], jnp.minimum(pair[1], slots - 1)]
            scores = dot_t(
                jnp.concatenate([held[here_slot[0]], held[here_slot[1]]], axis=0), units[o]
            )
            ok = jnp.where(lane < own_count, scores, absent)
            folded = jnp.maximum(
                jnp.maximum(ok[:, 0:128], ok[:, 128:256]), jnp.maximum(ok[:, 256:384], ok[:, 384:512])
            )
            top = row_out[o : o + 1, :]
            for half in range(2):
                span = slice(half * quarter, (half + 1) * quarter)
                here = jnp.where(part < plan[counts + pair[half]], scores[span], absent)
                top = jnp.maximum(top, jnp.max(here, axis=0, keepdims=True))
                cols[pl.ds(pair[half], 1), :] = jnp.max(folded[span].T, axis=0, keepdims=True)
            row_out[o : o + 1, :] = top
            return carry

        lax.fori_loop(0, (plan[base + o] + 1) >> 1, visit, 0)
    if final:
        outs[2][...] = row_out[blocks:]
        for slot in range(slots):
            number = len(every) - slots + slot
            col_out[pl.ds(plan[at_row + number], 1), :] = cols[slot : slot + 1, :]
    else:
        col_out[...] = cols[0:slots]


def spread_in(running, best, rep):
    wide = jnp.concatenate([best] * n_rep, axis=1)
    lane = lax.broadcasted_iota(jnp.int32, (blocks, rows), 1)
    mine = (lane >= rep * quarter) & (lane < (rep + 1) * quarter)
    return jnp.where(mine, jnp.maximum(running, wide), running)


def merge_kernel(plan, local, row_best, sib_rows, back, out, best):
    rep = lax.axis_index("rep")
    best[...] = jnp.full((blocks, quarter), absent, jnp.float32)
    for number in range(len(every)):
        block = plan[at_back + number]
        best[pl.ds(block, 1), :] = jnp.maximum(
            best[pl.ds(block, 1), :], back[pl.ds(plan[at_back_row + number], 1), :]
        )
    merged = jnp.maximum(jnp.maximum(local[...], row_best[0:blocks]), sib_rows[...])
    out[...] = spread_in(merged, best[...], rep)


def finish_kernel(plan, one, two, three, four, out):
    best = jnp.maximum(jnp.maximum(one[...], two[...]), jnp.maximum(three[...], four[...]))
    lane = lax.broadcasted_iota(jnp.int32, (1, quarter), 1)
    for b in range(blocks):
        count = plan[at_own + b]
        for q in range(n_rep):
            span = best[b : b + 1, q * quarter : (q + 1) * quarter]
            out[n_rep * b + q : n_rep * b + q + 1, :] = jnp.where(
                lane + q * quarter < count, span, -1.0
            )


def move(value, dx, dz):
    if dx % n_x == 0 and dz % n_z == 0:
        return value
    steps = [
        (x * n_z + z, (x + dx) % n_x * n_z + (z + dz) % n_z) for x in range(n_x) for z in range(n_z)
    ]
    return lax.ppermute(value, ("x", "z"), steps)


def on_device(embeddings, valid_rows, pair_table):
    smem = pl.BlockSpec(memory_space=pltpu.SMEM)
    vmem = pl.BlockSpec(memory_space=pltpu.VMEM)
    hbm = pl.BlockSpec(memory_space=pl.ANY)
    params = pltpu.CompilerParams(vmem_limit_bytes=vmem_bytes)
    cost = pl.CostEstimate(flops=0, bytes_accessed=1 << 16, transcendentals=0)
    f32, bf16 = jnp.float32, jnp.bfloat16
    part = (quarter, width)
    raw = embeddings.reshape(blocks, rows, width)

    def pick(wanted, spread, held, after, name):
        n = len(wanted)
        shapes = [(len(numbers),) + part for numbers in wanted]
        if spread:
            shapes = shapes[:-n_x] + [(n_x,) + shapes[-1]]
        return pl.pallas_call(
            functools.partial(pick_kernel, wanted, spread),
            out_shape=[jax.ShapeDtypeStruct(shape, bf16) for shape in shapes],
            in_specs=[smem] + [hbm] * len(held + after),
            out_specs=[hbm] * len(shapes),
            scratch_shapes=[
                pltpu.VMEM((n, 3) + part, bf16),
                pltpu.SemaphoreType.DMA((3 * n,)),
                pltpu.SemaphoreType.DMA((n,)),
            ],
            compiler_params=params,
            cost_estimate=cost,
            name=name,
        )(plan, *held, *after)

    def compare(stage, feeds, arrays, past, after, name):
        slots = len(stages[stage])
        shapes = [(2 * blocks, rows), (slots, quarter)]
        if past:
            shapes = [(2 * blocks, rows), (2 * chips, quarter), (blocks, rows)]
        return pl.pallas_call(
            functools.partial(pair_kernel, stage, feeds),
            out_shape=[jax.ShapeDtypeStruct(shape, f32) for shape in shapes],
            in_specs=[smem, hbm] + [vmem] * len(past) + [hbm] * len(arrays + after),
            out_specs=[vmem] * len(shapes),
            scratch_shapes=[
                pltpu.VMEM((2 * blocks, rows, width), bf16),
                pltpu.VMEM((slots,) + part, bf16),
                pltpu.VMEM((slots // 8 * 8 + 8, quarter), f32),
                pltpu.SemaphoreType.DMA((2 * blocks,)),
                pltpu.SemaphoreType.DMA((len(feeds),)),
            ],
            compiler_params=params,
            cost_estimate=cost,
            name=name,
        )(plan, units, *past, *arrays, *after)

    def numbers(wanted):
        return [[every.index(slot) for slot in slots] for slots in wanted]

    cols, *away, around = pl.pallas_call(
        prep_kernel,
        out_shape=[jax.ShapeDtypeStruct((blocks,) + part, bf16)]
        + [jax.ShapeDtypeStruct((1,) + part, bf16)] * n_x
        + [jax.ShapeDtypeStruct((2,) + part, bf16)],
        in_specs=[smem, hbm],
        out_specs=[hbm] * (2 + n_x),
        scratch_shapes=[
            pltpu.VMEM((blocks,) + part, bf16),
            pltpu.VMEM((blocks,) + part, bf16),
            pltpu.SemaphoreType.DMA((blocks,)),
            pltpu.SemaphoreType.DMA((len(far + down),)),
        ],
        compiler_params=params,
        cost_estimate=cost,
        name="prep",
    )(pair_table, raw)
    swap = [(0, 1), (1, 0)]
    sib_raw = lax.ppermute(raw, "core", swap)
    hop1 = move(cols, 0, 1)
    away = [move(a, dx, -2) for dx, a in enumerate(away)]
    plan = pl.pallas_call(
        plan_kernel,
        out_shape=jax.ShapeDtypeStruct((plan_size,), jnp.int32),
        in_specs=[smem, smem, hbm],
        out_specs=smem,
        compiler_params=params,
        cost_estimate=cost,
        name="plan",
    )(pair_table, valid_rows, cols)
    units, local_best = pl.pallas_call(
        local_kernel,
        grid=(2 * blocks,),
        out_shape=(
            jax.ShapeDtypeStruct((2 * blocks, rows, width), bf16),
            jax.ShapeDtypeStruct((blocks, rows), f32),
        ),
        in_specs=[
            smem,
            pl.BlockSpec((1, rows, width), lambda i: (jnp.minimum(i, blocks - 1), 0, 0)),
            pl.BlockSpec((1, rows, width), lambda i: (jnp.maximum(i - blocks, 0), 0, 0)),
            pl.BlockSpec((blocks,) + part, lambda i: (0, 0, 0)),
        ],
        out_specs=(
            pl.BlockSpec((1, rows, width), lambda i: (i, 0, 0)),
            pl.BlockSpec((blocks, rows), lambda i: (0, 0)),
        ),
        compiler_params=params,
        cost_estimate=cost,
        name="local",
    )(valid_rows, raw, sib_raw, cols)
    hop1, away, local_best, plan = lax.optimization_barrier((hop1, away, local_best, plan))
    hop2 = move(hop1, 0, 1)
    away = move(jnp.concatenate(away, axis=0), 0, -2)
    picked = pick(numbers(first), False, [cols, hop1], [], "pick_a")
    first_in = [move(a, dx, 0) for dx, a in enumerate(picked)]
    hop2, away, around = lax.optimization_barrier((hop2, away, around))
    picked = pick(numbers(third + second), True, [cols, hop2], first_in, "pick_b")
    third_in = [move(a, slots[0][0], 1) for slots, a in zip(third, picked)]
    second_in = lax.all_to_all(picked[-1], "x", split_axis=0, concat_axis=0, tiled=True)
    down_in = move(around, 2, -3)

    past_a = compare(
        0,
        [(dx, None, 3, 3 * dx) for dx in range(n_x)] + [(n_x, None, n_x, 3 * n_x)],
        first_in + [away],
        [],
        [picked[0]],
        "pairs_a",
    )
    past_b = compare(
        1,
        [(0, None, 2, 0), (1, None, 2, 2)],
        third_in[:2],
        [],
        [past_a[0]],
        "pairs_b",
    )
    row_best, col_best, sib_best = compare(
        2,
        [(0, None, 2, 0), (1, None, 2, 2)] + [(2, dx, 2, 4 + 2 * dx) for dx in range(n_x)],
        [third_in[2], down_in, second_in],
        [*past_a, *past_b],
        [],
        "pairs_c",
    )
    sib_rows = lax.ppermute(sib_best, "core", swap)
    back = lax.all_to_all(col_best, ("x", "z"), split_axis=0, concat_axis=0, tiled=True)
    combined = pl.pallas_call(
        merge_kernel,
        out_shape=jax.ShapeDtypeStruct((blocks, rows), f32),
        in_specs=[smem, vmem, vmem, vmem, vmem],
        out_specs=vmem,
        scratch_shapes=[pltpu.VMEM((blocks, quarter), f32)],
        cost_estimate=cost,
        name="merge",
    )(plan, local_best, row_best, sib_rows, back)
    others = [
        lax.ppermute(combined, "rep", [(y, (y + d) % n_rep) for y in range(n_rep)])
        for d in range(1, n_rep)
    ]
    result = pl.pallas_call(
        finish_kernel,
        out_shape=jax.ShapeDtypeStruct((blocks * n_rep, quarter), f32),
        in_specs=[smem, vmem, vmem, vmem, vmem],
        out_specs=vmem,
        cost_estimate=cost,
        name="finish",
    )(plan, combined, *others)
    return result.reshape(-1)


def solution(mesh):
    grid = Mesh(mesh.devices.reshape(n_x, n_z, n_core, n_rep), ("x", "z", "core", "rep"))
    return jax.shard_map(
        on_device,
        mesh=grid,
        in_specs=(P(("x", "z", "core"), None), P(), P()),
        out_specs=P(("x", "z", "core")),
        check_vma=False,
    )
```

```python
import functools

import jax
import jax.numpy as jnp
from jax import lax
from jax.experimental import pallas as pl
from jax.experimental.pallas import tpu as pltpu
from jax.sharding import Mesh, PartitionSpec as P

absent = -2.0
epsilon = 1e-06
n_x, n_z, n_core, n_rep = 4, 8, 2, 4
chips = n_x * n_z
blocks = 8
rows = 512
quarter = rows // n_rep
width = 768
vmem_bytes = 60 << 20


def dot_t(left, right):
    return lax.dot_general(
        left, right, (((1,), (1,)), ((), ())), preferred_element_type=jnp.float32
    )


def normalise(raw):
    wide = raw.astype(jnp.float32)
    scale = lax.rsqrt(jnp.sum(wide * wide, axis=-1, keepdims=True) + epsilon)
    return (wide * scale).astype(jnp.bfloat16)


def place():
    return lax.axis_index("x"), lax.axis_index("z"), lax.axis_index("core"), lax.axis_index("rep")


def pair_info(table, source, target, core, many, which):
    side = which if many == 2 else jnp.where(source < target, core, 1 - core)
    forth = table[source * n_core + core, target * n_core + side]
    back = table[target * n_core + side, source * n_core + core]
    live = (forth >= 0) | (back >= 0)
    if many == 1:
        live = live & ((source != target) | (core == 0))
    source_block = jnp.where(forth >= 0, forth >> 3, back & 7)
    target_block = jnp.where(forth >= 0, forth & 7, (back >> 3) & 7)
    return live, side, source_block, target_block


def chip_at(x, z, dx, dz):
    return ((x + dx + n_x) & (n_x - 1)) * n_z + ((z + dz + n_z) & (n_z - 1))


first = [[(dx, 0, 1, 0), (dx, 1, 2, 0), (dx, 1, 2, 1)] for dx in range(n_x)]
second = [[(dx, 2, 2, 0), (dx, 2, 2, 1)] for dx in range(n_x)]
third = [[(dx, 3, 2, 0), (dx, 3, 2, 1)] for dx in (0, 1, 3)]
far = [(dx, 4, 1, 0) for dx in range(n_x)]
down = [(2, 5, 2, 0), (2, 5, 2, 1)]
stages = [sum(first, []) + far, third[0] + third[1], third[2] + down + sum(second, [])]
every = sum(stages, [])
gone_of = {0: 0, 1: 1, 2: 2, 3: 2}
at_pick, at_back, at_back_row, at_row, at_own = 0, 32, 64, 96, 128
at_stage, plan_size = [], 144
for stage in stages:
    at_stage.append(plan_size)
    plan_size += 16 + len(stage) + 1 + 1 + 3 * (len(stage) + 2)


def places(stage, base):
    slots = len(stage)
    counts = base + 2 * blocks
    groups = counts + slots + 1
    own_of = groups + 1
    return counts, groups, own_of, own_of + slots + 2, own_of + 2 * (slots + 2)


def plan_kernel(table, valid, after, plan, latest):
    x, z, core, rep = place()
    chip = chip_at(x, z, 0, 0)
    start = rep * quarter
    for o in range(2 * blocks):
        owner = chip * n_core + (core if o < blocks else 1 - core)
        plan[at_own + o] = valid[owner * blocks + o % blocks]
    number = 0
    for stage, base in zip(stages, at_stage):
        slots = len(stage)
        counts, groups, own_of, first_of, second_of = places(stage, base)
        for o in range(2 * blocks):
            plan[base + o] = 0
            latest[o] = 0
        plan[groups] = 0
        for slot, (dx, dz, many, which) in enumerate(stage):
            target = chip_at(x, z, dx, dz)
            _, _, block, _ = pair_info(table, chip, target, core, many, which)
            plan[at_back + number] = block
            plan[at_back_row + number] = 2 * target + which
            if dz in gone_of:
                gone = gone_of[dz]
                source, target = chip_at(x, z, 0, -gone), chip_at(x, z, dx, dz - gone)
                _, _, block, _ = pair_info(table, source, target, core, many, which)
                plan[at_pick + number] = block
            source = chip_at(x, z, -dx, -dz)
            live, side, block, own_block = pair_info(table, source, chip, core, many, which)
            mine = jnp.where(side == core, 0, blocks) + own_block
            count = plan[groups]
            joins = (plan[base + mine] & 1) == 1
            group = jnp.where(live, jnp.where(joins, latest[mine], count), slots + 1)
            plan[own_of + group] = mine
            plan[first_of + group] = jnp.where(joins, plan[first_of + group], slot)
            plan[second_of + group] = jnp.where(joins, slot, slots)
            latest[mine] = jnp.where(live, group, latest[mine])
            plan[groups] = count + (live & jnp.logical_not(joins)).astype(jnp.int32)
            plan[base + mine] = plan[base + mine] + live.astype(jnp.int32)
            plan[counts + slot] = valid[(source * n_core + core) * blocks + block] - start
            plan[at_row + number] = 2 * source + which
            number += 1
        plan[counts + slots] = 0
        count = plan[groups]
        plan[own_of + count] = plan[own_of]
        plan[first_of + count] = slots
        plan[second_of + count] = slots


def prep_kernel(table, emb, units, to0, to1, to2, to3, around, raw, unit, sem_in, sems):
    x, z, core, rep = place()
    chip = chip_at(x, z, 0, 0)
    loads = [
        pltpu.make_async_copy(emb.at[b, pl.ds(rep * quarter, quarter)], raw.at[b], sem_in.at[b])
        for b in range(blocks)
    ]
    for load in loads:
        load.start()
    copies = []
    for b in range(blocks):
        loads[b].wait()
        unit[b] = normalise(raw[b])
        copies.append(pltpu.make_async_copy(unit.at[b], units.at[b], sem_in.at[b]))
        copies[-1].start()
    outs = [to0.at[0], to1.at[0], to2.at[0], to3.at[0], around.at[0], around.at[1]]
    for a, (dx, dz, many, which) in enumerate(far + down):
        _, _, block, _ = pair_info(table, chip, chip_at(x, z, dx, dz), core, many, which)
        copies.append(pltpu.make_async_copy(unit.at[block], outs[a], sems.at[a]))
        copies[-1].start()
    for copy in copies:
        copy.wait()


def pick_kernel(wanted, spread, plan, *refs):
    near_by, hop = refs[:2]
    parts, get_sems, put_sems = refs[-3:]
    x, z, core, rep = place()
    n = len(wanted)
    if spread:
        outs = list(refs[-n + n_x - 4 : -4])
        outs += [refs[-4].at[(x + dx) & (n_x - 1)] for dx in range(n_x)]
    else:
        outs = refs[-n - 3 : -3]
    gets, puts = [], []
    for a, numbers in enumerate(wanted):
        for place_in, number in enumerate(numbers):
            held = near_by if every[number][1] == 0 else hop
            gets.append(
                pltpu.make_async_copy(
                    held.at[plan[at_pick + number]],
                    parts.at[a, place_in],
                    get_sems.at[3 * a + place_in],
                )
            )
            gets[-1].start()
    left = list(gets)
    for a, (out, numbers) in enumerate(zip(outs, wanted)):
        for _ in numbers:
            left.pop(0).wait()
        puts.append(
            pltpu.make_async_copy(parts.at[a, pl.ds(0, len(numbers))], out, put_sems.at[a])
        )
        puts[-1].start()
    for copy in puts:
        copy.wait()


def local_kernel(valid, own, sib, cols, unit_out, best):
    step = pl.program_id(0)
    x, z, core, rep = place()
    dev = chip_at(x, z, 0, 0) * n_core + core
    start = rep * quarter

    @pl.when(step >= blocks)
    def _():
        unit_out[0] = normalise(sib[0])

    @pl.when(step < blocks)
    def _():
        mine = normalise(own[0])
        unit_out[0] = mine
        part = lax.broadcasted_iota(jnp.int32, (quarter, rows), 0)
        gap = lax.broadcasted_iota(jnp.int32, (quarter, rows), 1) - part
        found = jnp.full((1, rows), absent, jnp.float32)
        for k in range(0, blocks, 2):
            pair = jnp.concatenate([cols[k], cols[k + 1]], axis=0)
            scores = dot_t(pair, mine)
            for half in range(2):
                count = valid[dev * blocks + k + half] - start
                own_gap = jnp.where(k + half == step, start, rows)
                allowed = (part < count) & (gap != own_gap)
                here = jnp.where(allowed, scores[half * quarter : (half + 1) * quarter], absent)
                found = jnp.maximum(found, jnp.max(here, axis=0, keepdims=True))
        best[pl.ds(step, 1), :] = found


def pair_kernel(stage, feeds, plan, own, *refs):
    final = stage == len(stages) - 1
    slots, base = len(stages[stage]), at_stage[stage]
    counts, groups, own_of, first_of, second_of = places(stages[stage], base)
    units, held, cols, sem_u, sem_g = refs[-5:]
    outs, arrays, past = refs[-8 if final else -7 : -5], refs, ()
    if final:
        past, arrays = refs[: 2 * stage], refs[2 * stage :]
    x, z, core, rep = place()
    gets = []
    for a, (array, dx, count, first_slot) in enumerate(feeds):
        came = arrays[array] if dx is None else arrays[array].at[(x - dx + n_x) & (n_x - 1)]
        gets.append(pltpu.make_async_copy(came, held.at[pl.ds(first_slot, count)], sem_g.at[a]))
        gets[-1].start()
    loads = []
    for o in range(2 * blocks):
        loads.append(pltpu.make_async_copy(own.at[o], units.at[o], sem_u.at[o]))

        @pl.when(plan[base + o] > 0)
        def _():
            loads[o].start()

    row_out, col_out = outs[:2]
    row_out[...] = jnp.full((2 * blocks, rows), absent, jnp.float32)
    for ref in past[::2]:
        row_out[...] = jnp.maximum(row_out[...], ref[...])
    cols[...] = jnp.full(cols.shape, absent, jnp.float32)
    if final:
        col_out[...] = jnp.full(col_out.shape, absent, jnp.float32)
        number = 0
        for ref, done in zip(past[1::2], stages):
            for slot in range(len(done)):
                col_out[pl.ds(plan[at_row + number], 1), :] = ref[slot : slot + 1, :]
                number += 1
    part = lax.broadcasted_iota(jnp.int32, (quarter, rows), 0)
    lane = lax.broadcasted_iota(jnp.int32, (2 * quarter, rows), 1)
    for copy in gets:
        copy.wait()
    for o in range(2 * blocks):

        @pl.when(plan[base + o] > 0)
        def _():
            loads[o].wait()

    def visit(turn, carry):
        for group in (2 * turn, 2 * turn + 1):
            o = plan[own_of + group]
            pair = [plan[first_of + group], plan[second_of + group]]
            here_slot = [jnp.minimum(slot, slots - 1) for slot in pair]
            scores = dot_t(
                jnp.concatenate([held[here_slot[0]], held[here_slot[1]]], axis=0), units[o]
            )
            ok = jnp.where(lane < plan[at_own + o], scores, absent)
            folded = jnp.maximum(
                jnp.maximum(ok[:, 0:128], ok[:, 128:256]), jnp.maximum(ok[:, 256:384], ok[:, 384:512])
            )
            top = jnp.full((1, rows), absent, jnp.float32)
            for half in range(2):
                span = slice(half * quarter, (half + 1) * quarter)
                here = jnp.where(part < plan[counts + pair[half]], scores[span], absent)
                top = jnp.maximum(top, jnp.max(here, axis=0, keepdims=True))
                cols[pl.ds(pair[half], 1), :] = jnp.max(folded[span].T, axis=0, keepdims=True)
            row_out[pl.ds(o, 1), :] = jnp.maximum(row_out[pl.ds(o, 1), :], top)
        return carry

    lax.fori_loop(0, (plan[groups] + 1) >> 1, visit, 0)
    if final:
        outs[2][...] = row_out[blocks:]
        for slot in range(slots):
            number = len(every) - slots + slot
            col_out[pl.ds(plan[at_row + number], 1), :] = cols[slot : slot + 1, :]
    else:
        col_out[...] = cols[0:slots]


def spread_in(running, best, rep):
    wide = jnp.concatenate([best] * n_rep, axis=1)
    lane = lax.broadcasted_iota(jnp.int32, (blocks, rows), 1)
    mine = (lane >= rep * quarter) & (lane < (rep + 1) * quarter)
    return jnp.where(mine, jnp.maximum(running, wide), running)


def merge_kernel(plan, local, row_best, sib_rows, back, out, best):
    rep = lax.axis_index("rep")
    best[...] = jnp.full((blocks, quarter), absent, jnp.float32)
    for number in range(len(every)):
        block = plan[at_back + number]
        best[pl.ds(block, 1), :] = jnp.maximum(
            best[pl.ds(block, 1), :], back[pl.ds(plan[at_back_row + number], 1), :]
        )
    merged = jnp.maximum(jnp.maximum(local[...], row_best[0:blocks]), sib_rows[...])
    merged = spread_in(merged, best[...], rep)
    lane = lax.broadcasted_iota(jnp.int32, (1, rows), 1)
    for b in range(blocks):
        out[b : b + 1, :] = jnp.where(lane < plan[at_own + b], merged[b : b + 1], -1.0)


def finish_kernel(one, two, three, four, out):
    best = jnp.maximum(jnp.maximum(one[...], two[...]), jnp.maximum(three[...], four[...]))
    for b in range(blocks):
        for q in range(n_rep):
            out[n_rep * b + q : n_rep * b + q + 1, :] = best[
                b : b + 1, q * quarter : (q + 1) * quarter
            ]


def move(value, dx, dz):
    if dx % n_x == 0 and dz % n_z == 0:
        return value
    steps = [
        (x * n_z + z, (x + dx) % n_x * n_z + (z + dz) % n_z) for x in range(n_x) for z in range(n_z)
    ]
    return lax.ppermute(value, ("x", "z"), steps)


def on_device(embeddings, valid_rows, pair_table):
    smem = pl.BlockSpec(memory_space=pltpu.SMEM)
    vmem = pl.BlockSpec(memory_space=pltpu.VMEM)
    hbm = pl.BlockSpec(memory_space=pl.ANY)
    pinned = pl.BlockSpec(memory_space=pltpu.HBM)
    params = pltpu.CompilerParams(vmem_limit_bytes=vmem_bytes)
    middle = pltpu.CompilerParams(vmem_limit_bytes=56 << 20)
    small = pltpu.CompilerParams(vmem_limit_bytes=8 << 20)
    cost = pl.CostEstimate(flops=0, bytes_accessed=1 << 16, transcendentals=0)
    f32, bf16 = jnp.float32, jnp.bfloat16
    part = (quarter, width)
    raw = embeddings.reshape(blocks, rows, width)

    def pick(wanted, spread, held, after, name):
        n = len(wanted)
        shapes = [(len(numbers),) + part for numbers in wanted]
        if spread:
            shapes = shapes[:-n_x] + [(n_x,) + shapes[-1]]
        return pl.pallas_call(
            functools.partial(pick_kernel, wanted, spread),
            out_shape=[jax.ShapeDtypeStruct(shape, bf16) for shape in shapes],
            in_specs=[smem] + [hbm] * len(held + after),
            out_specs=[hbm] * len(shapes),
            scratch_shapes=[
                pltpu.VMEM((n, 3) + part, bf16),
                pltpu.SemaphoreType.DMA((3 * n,)),
                pltpu.SemaphoreType.DMA((n,)),
            ],
            compiler_params=middle,
            cost_estimate=cost,
            name=name,
        )(plan, *held, *after)

    def compare(stage, feeds, arrays, past, after, name):
        slots = len(stages[stage])
        shapes = [(2 * blocks, rows), (slots, quarter)]
        if past:
            shapes = [(2 * blocks, rows), (2 * chips, quarter), (blocks, rows)]
        return pl.pallas_call(
            functools.partial(pair_kernel, stage, feeds),
            out_shape=[jax.ShapeDtypeStruct(shape, f32) for shape in shapes],
            in_specs=[smem, pinned] + [vmem] * len(past) + [hbm] * len(arrays + after),
            out_specs=[vmem] * len(shapes),
            scratch_shapes=[
                pltpu.VMEM((2 * blocks, rows, width), bf16),
                pltpu.VMEM((slots,) + part, bf16),
                pltpu.VMEM((slots // 8 * 8 + 8, quarter), f32),
                pltpu.SemaphoreType.DMA((2 * blocks,)),
                pltpu.SemaphoreType.DMA((len(feeds),)),
            ],
            compiler_params=middle,
            cost_estimate=cost,
            name=name,
        )(plan, units, *past, *arrays, *after)

    def numbers(wanted):
        return [[every.index(slot) for slot in slots] for slots in wanted]

    cols, *away, around = pl.pallas_call(
        prep_kernel,
        out_shape=[jax.ShapeDtypeStruct((blocks,) + part, bf16)]
        + [jax.ShapeDtypeStruct((1,) + part, bf16)] * n_x
        + [jax.ShapeDtypeStruct((2,) + part, bf16)],
        in_specs=[smem, hbm],
        out_specs=[hbm] * (2 + n_x),
        scratch_shapes=[
            pltpu.VMEM((blocks,) + part, bf16),
            pltpu.VMEM((blocks,) + part, bf16),
            pltpu.SemaphoreType.DMA((blocks,)),
            pltpu.SemaphoreType.DMA((len(far + down),)),
        ],
        compiler_params=params,
        cost_estimate=cost,
        name="prep",
    )(pair_table, raw)
    swap = [(0, 1), (1, 0)]
    sib_raw = lax.ppermute(raw, "core", swap)
    hop1 = move(cols, 0, 1)
    away = [move(a, dx, -2) for dx, a in enumerate(away)]
    plan = pl.pallas_call(
        plan_kernel,
        out_shape=jax.ShapeDtypeStruct((plan_size,), jnp.int32),
        in_specs=[smem, smem, hbm],
        out_specs=smem,
        scratch_shapes=[pltpu.SMEM((2 * blocks,), jnp.int32)],
        compiler_params=params,
        cost_estimate=cost,
        name="plan",
    )(pair_table, valid_rows, cols)
    units, local_best = pl.pallas_call(
        local_kernel,
        grid=(2 * blocks,),
        out_shape=(
            jax.ShapeDtypeStruct((2 * blocks, rows, width), bf16),
            jax.ShapeDtypeStruct((blocks, rows), f32),
        ),
        in_specs=[
            smem,
            pl.BlockSpec((1, rows, width), lambda i: (jnp.minimum(i, blocks - 1), 0, 0)),
            pl.BlockSpec((1, rows, width), lambda i: (jnp.maximum(i - blocks, 0), 0, 0)),
            pl.BlockSpec((blocks,) + part, lambda i: (0, 0, 0)),
        ],
        out_specs=(
            pl.BlockSpec((1, rows, width), lambda i: (i, 0, 0)),
            pl.BlockSpec((blocks, rows), lambda i: (0, 0)),
        ),
        compiler_params=params,
        cost_estimate=cost,
        name="local",
    )(valid_rows, raw, sib_raw, cols)
    hop1, away, local_best, plan = lax.optimization_barrier((hop1, away, local_best, plan))
    hop2 = move(hop1, 0, 1)
    away = move(jnp.concatenate(away, axis=0), 0, -2)
    picked = pick(numbers(first), False, [cols, hop1], [], "pick_a")
    first_in = [move(a, dx, 0) for dx, a in enumerate(picked)]
    hop2, away, around = lax.optimization_barrier((hop2, away, around))
    picked = pick(numbers(third + second), True, [cols, hop2], first_in, "pick_b")
    third_in = [move(a, slots[0][0], 1) for slots, a in zip(third, picked)]
    second_in = lax.all_to_all(picked[-1], "x", split_axis=0, concat_axis=0, tiled=True)
    down_in = move(around, 2, -3)

    past_a = compare(
        0,
        [(dx, None, 3, 3 * dx) for dx in range(n_x)] + [(n_x, None, n_x, 3 * n_x)],
        first_in + [away],
        [],
        [picked[0]],
        "pairs_a",
    )
    past_b = compare(
        1,
        [(0, None, 2, 0), (1, None, 2, 2)],
        third_in[:2],
        [],
        [past_a[0]],
        "pairs_b",
    )
    row_best, col_best, sib_best = compare(
        2,
        [(0, None, 2, 0), (1, None, 2, 2)] + [(2, dx, 2, 4 + 2 * dx) for dx in range(n_x)],
        [third_in[2], down_in, second_in],
        [*past_a, *past_b],
        [],
        "pairs_c",
    )
    sib_rows = lax.ppermute(sib_best, "core", swap)
    back = lax.all_to_all(col_best, ("x", "z"), split_axis=0, concat_axis=0, tiled=True)
    combined = pl.pallas_call(
        merge_kernel,
        out_shape=jax.ShapeDtypeStruct((blocks, rows), f32),
        in_specs=[smem, vmem, vmem, vmem, vmem],
        out_specs=vmem,
        scratch_shapes=[pltpu.VMEM((blocks, quarter), f32)],
        compiler_params=small,
        cost_estimate=cost,
        name="merge",
    )(plan, local_best, row_best, sib_rows, back)
    others = [
        lax.ppermute(combined, "rep", [(y, (y + d) % n_rep) for y in range(n_rep)])
        for d in range(1, n_rep)
    ]
    result = pl.pallas_call(
        finish_kernel,
        out_shape=jax.ShapeDtypeStruct((blocks * n_rep, quarter), f32),
        in_specs=[vmem, vmem, vmem, vmem],
        out_specs=vmem,
        compiler_params=small,
        cost_estimate=cost,
        name="finish",
    )(combined, *others)
    return result.reshape(-1)


def solution(mesh):
    grid = Mesh(mesh.devices.reshape(n_x, n_z, n_core, n_rep), ("x", "z", "core", "rep"))
    return jax.shard_map(
        on_device,
        mesh=grid,
        in_specs=(P(("x", "z", "core"), None), P(), P()),
        out_specs=P(("x", "z", "core")),
        check_vma=False,
    )
```

```python
import functools

import jax
import jax.numpy as jnp
from jax import lax
from jax.experimental import pallas as pl
from jax.experimental.pallas import tpu as pltpu
from jax.sharding import Mesh, PartitionSpec as P

absent = -2.0
epsilon = 1e-06
n_x, n_z, n_core, n_rep = 4, 8, 2, 4
chips = n_x * n_z
blocks = 8
rows = 512
quarter = rows // n_rep
width = 768
vmem_bytes = 60 << 20


def dot_t(left, right):
    return lax.dot_general(
        left, right, (((1,), (1,)), ((), ())), preferred_element_type=jnp.float32
    )


def normalise(raw):
    wide = raw.astype(jnp.float32)
    scale = lax.rsqrt(jnp.sum(wide * wide, axis=-1, keepdims=True) + epsilon)
    return (wide * scale).astype(jnp.bfloat16)


def place():
    return lax.axis_index("x"), lax.axis_index("z"), lax.axis_index("core"), lax.axis_index("rep")


def pair_info(table, source, target, core, many, which):
    side = which if many == 2 else jnp.where(source < target, core, 1 - core)
    forth = table[source * n_core + core, target * n_core + side]
    back = table[target * n_core + side, source * n_core + core]
    live = (forth >= 0) | (back >= 0)
    if many == 1:
        live = live & ((source != target) | (core == 0))
    source_block = jnp.where(forth >= 0, forth >> 3, back & 7)
    target_block = jnp.where(forth >= 0, forth & 7, (back >> 3) & 7)
    return live, side, source_block, target_block


def chip_at(x, z, dx, dz):
    return ((x + dx + n_x) & (n_x - 1)) * n_z + ((z + dz + n_z) & (n_z - 1))


first = [[(dx, 0, 1, 0), (dx, 1, 2, 0), (dx, 1, 2, 1)] for dx in range(n_x)]
second = [[(dx, 2, 2, 0), (dx, 2, 2, 1)] for dx in range(n_x)]
third = [[(dx, 3, 2, 0), (dx, 3, 2, 1)] for dx in (0, 1, 3)]
far = [(dx, 4, 1, 0) for dx in range(n_x)]
down = [(2, 5, 2, 0), (2, 5, 2, 1)]
stages = [sum(first, []) + far, third[0] + third[1], third[2] + down + sum(second, [])]
every = sum(stages, [])
gone_of = {0: 0, 1: 1, 2: 2, 3: 2}
at_pick, at_back, at_back_row, at_row, at_own = 0, 32, 64, 96, 128
at_stage, plan_size = [], 144
for stage in stages:
    at_stage.append(plan_size)
    plan_size += 16 + len(stage) + 1 + 1 + 4 * (len(stage) + 2)


def places(stage, base):
    slots = len(stage)
    counts = base + 2 * blocks
    groups = counts + slots + 1
    own_of = groups + 1
    return counts, groups, own_of, *(own_of + k * (slots + 2) for k in (1, 2, 3))


def plan_kernel(table, valid, after, plan, latest):
    x, z, core, rep = place()
    chip = chip_at(x, z, 0, 0)
    start = rep * quarter
    for o in range(2 * blocks):
        owner = chip * n_core + (core if o < blocks else 1 - core)
        plan[at_own + o] = valid[owner * blocks + o % blocks]
    number = 0
    for stage, base in zip(stages, at_stage):
        slots = len(stage)
        counts, groups, own_of, first_of, second_of, fresh_of = places(stage, base)
        for o in range(2 * blocks):
            plan[base + o] = 0
            latest[o] = 0
        plan[groups] = 0
        for slot, (dx, dz, many, which) in enumerate(stage):
            target = chip_at(x, z, dx, dz)
            _, _, block, _ = pair_info(table, chip, target, core, many, which)
            plan[at_back + number] = block
            plan[at_back_row + number] = 2 * target + which
            if dz in gone_of:
                gone = gone_of[dz]
                source, target = chip_at(x, z, 0, -gone), chip_at(x, z, dx, dz - gone)
                _, _, block, _ = pair_info(table, source, target, core, many, which)
                plan[at_pick + number] = block
            source = chip_at(x, z, -dx, -dz)
            live, side, block, own_block = pair_info(table, source, chip, core, many, which)
            mine = jnp.where(side == core, 0, blocks) + own_block
            count = plan[groups]
            joins = (plan[base + mine] & 1) == 1
            group = jnp.where(live, jnp.where(joins, latest[mine], count), slots + 1)
            plan[own_of + group] = mine
            fresh = (plan[base + mine] == 0).astype(jnp.int32)
            plan[fresh_of + group] = jnp.where(joins, plan[fresh_of + group], fresh)
            plan[first_of + group] = jnp.where(joins, plan[first_of + group], slot)
            plan[second_of + group] = jnp.where(joins, slot, slots)
            latest[mine] = jnp.where(live, group, latest[mine])
            plan[groups] = count + (live & jnp.logical_not(joins)).astype(jnp.int32)
            plan[base + mine] = plan[base + mine] + live.astype(jnp.int32)
            plan[counts + slot] = valid[(source * n_core + core) * blocks + block] - start
            plan[at_row + number] = 2 * source + which
            number += 1
        plan[counts + slots] = 0
        count = plan[groups]
        plan[own_of + count] = plan[own_of]
        plan[first_of + count] = slots
        plan[fresh_of + count] = 0
        plan[second_of + count] = slots


def prep_kernel(table, emb, units, to0, to1, to2, to3, around, raw, unit, sem_in, sems):
    x, z, core, rep = place()
    chip = chip_at(x, z, 0, 0)
    loads = [
        pltpu.make_async_copy(emb.at[b, pl.ds(rep * quarter, quarter)], raw.at[b], sem_in.at[b])
        for b in range(blocks)
    ]
    for load in loads:
        load.start()
    copies = []
    for b in range(blocks):
        loads[b].wait()
        unit[b] = normalise(raw[b])
        copies.append(pltpu.make_async_copy(unit.at[b], units.at[b], sem_in.at[b]))
        copies[-1].start()
    outs = [to0.at[0], to1.at[0], to2.at[0], to3.at[0], around.at[0], around.at[1]]
    for a, (dx, dz, many, which) in enumerate(far + down):
        _, _, block, _ = pair_info(table, chip, chip_at(x, z, dx, dz), core, many, which)
        copies.append(pltpu.make_async_copy(unit.at[block], outs[a], sems.at[a]))
        copies[-1].start()
    for copy in copies:
        copy.wait()


def pick_kernel(wanted, spread, plan, *refs):
    near_by, hop = refs[:2]
    parts, get_sems, put_sems = refs[-3:]
    x, z, core, rep = place()
    n = len(wanted)
    if spread:
        outs = list(refs[-n + n_x - 4 : -4])
        outs += [refs[-4].at[(x + dx) & (n_x - 1)] for dx in range(n_x)]
    else:
        outs = refs[-n - 3 : -3]
    gets, puts = [], []
    for a, numbers in enumerate(wanted):
        for place_in, number in enumerate(numbers):
            held = near_by if every[number][1] == 0 else hop
            gets.append(
                pltpu.make_async_copy(
                    held.at[plan[at_pick + number]],
                    parts.at[a, place_in],
                    get_sems.at[3 * a + place_in],
                )
            )
            gets[-1].start()
    left = list(gets)
    for a, (out, numbers) in enumerate(zip(outs, wanted)):
        for _ in numbers:
            left.pop(0).wait()
        puts.append(
            pltpu.make_async_copy(parts.at[a, pl.ds(0, len(numbers))], out, put_sems.at[a])
        )
        puts[-1].start()
    for copy in puts:
        copy.wait()


def local_kernel(valid, own, sib, cols, unit_out, best):
    step = pl.program_id(0)
    x, z, core, rep = place()
    dev = chip_at(x, z, 0, 0) * n_core + core
    start = rep * quarter

    @pl.when(step >= blocks)
    def _():
        unit_out[0] = normalise(sib[0])

    @pl.when(step < blocks)
    def _():
        mine = normalise(own[0])
        unit_out[0] = mine
        part = lax.broadcasted_iota(jnp.int32, (quarter, rows), 0)
        gap = lax.broadcasted_iota(jnp.int32, (quarter, rows), 1) - part
        found = jnp.full((1, rows), absent, jnp.float32)
        for k in range(0, blocks, 2):
            pair = jnp.concatenate([cols[k], cols[k + 1]], axis=0)
            scores = dot_t(pair, mine)
            for half in range(2):
                count = valid[dev * blocks + k + half] - start
                own_gap = jnp.where(k + half == step, start, rows)
                allowed = (part < count) & (gap != own_gap)
                here = jnp.where(allowed, scores[half * quarter : (half + 1) * quarter], absent)
                found = jnp.maximum(found, jnp.max(here, axis=0, keepdims=True))
        best[pl.ds(step, 1), :] = found


def pair_kernel(stage, feeds, plan, own, *refs):
    final = stage == len(stages) - 1
    slots, base = len(stages[stage]), at_stage[stage]
    counts, groups, own_of, first_of, second_of, fresh_of = places(stages[stage], base)
    units, held, cols, sem_u, sem_g = refs[-5:]
    outs, arrays, past = refs[-8 if final else -7 : -5], refs, ()
    if final:
        past, arrays = refs[: 2 * stage], refs[2 * stage :]
    x, z, core, rep = place()
    gets = []
    for a, (array, dx, count, first_slot) in enumerate(feeds):
        came = arrays[array] if dx is None else arrays[array].at[(x - dx + n_x) & (n_x - 1)]
        gets.append(pltpu.make_async_copy(came, held.at[pl.ds(first_slot, count)], sem_g.at[a]))
        gets[-1].start()
    loads = []
    for o in range(2 * blocks):
        loads.append(pltpu.make_async_copy(own.at[o], units.at[o], sem_u.at[o]))

        @pl.when(plan[base + o] > 0)
        def _():
            loads[o].start()

    row_out, col_out = outs[:2]
    row_out[...] = jnp.full((2 * blocks, rows), absent, jnp.float32)
    for ref in past[::2]:
        row_out[...] = jnp.maximum(row_out[...], ref[...])
    cols[...] = jnp.full(cols.shape, absent, jnp.float32)
    if final:
        col_out[...] = jnp.full(col_out.shape, absent, jnp.float32)
        number = 0
        for ref, done in zip(past[1::2], stages):
            for slot in range(len(done)):
                col_out[pl.ds(plan[at_row + number], 1), :] = ref[slot : slot + 1, :]
                number += 1
    part = lax.broadcasted_iota(jnp.int32, (quarter, rows), 0)
    lane = lax.broadcasted_iota(jnp.int32, (2 * quarter, rows), 1)
    for copy in gets:
        copy.wait()

    def visit(turn, carry):
        for group in (2 * turn, 2 * turn + 1):

            @pl.when(plan[fresh_of + group] == 1)
            def _():
                o = plan[own_of + group]
                pltpu.make_async_copy(own.at[o], units.at[o], sem_u.at[o]).wait()

        for group in (2 * turn, 2 * turn + 1):
            o = plan[own_of + group]
            pair = [plan[first_of + group], plan[second_of + group]]
            here_slot = [jnp.minimum(slot, slots - 1) for slot in pair]
            scores = dot_t(
                jnp.concatenate([held[here_slot[0]], held[here_slot[1]]], axis=0), units[o]
            )
            ok = jnp.where(lane < plan[at_own + o], scores, absent)
            folded = jnp.maximum(
                jnp.maximum(ok[:, 0:128], ok[:, 128:256]), jnp.maximum(ok[:, 256:384], ok[:, 384:512])
            )
            top = jnp.full((1, rows), absent, jnp.float32)
            for half in range(2):
                span = slice(half * quarter, (half + 1) * quarter)
                here = jnp.where(part < plan[counts + pair[half]], scores[span], absent)
                top = jnp.maximum(top, jnp.max(here, axis=0, keepdims=True))
                cols[pl.ds(pair[half], 1), :] = jnp.max(folded[span].T, axis=0, keepdims=True)
            row_out[pl.ds(o, 1), :] = jnp.maximum(row_out[pl.ds(o, 1), :], top)
        return carry

    lax.fori_loop(0, (plan[groups] + 1) >> 1, visit, 0)
    if final:
        outs[2][...] = row_out[blocks:]
        for slot in range(slots):
            number = len(every) - slots + slot
            col_out[pl.ds(plan[at_row + number], 1), :] = cols[slot : slot + 1, :]
    else:
        col_out[...] = cols[0:slots]


def spread_in(running, best, rep):
    wide = jnp.concatenate([best] * n_rep, axis=1)
    lane = lax.broadcasted_iota(jnp.int32, (blocks, rows), 1)
    mine = (lane >= rep * quarter) & (lane < (rep + 1) * quarter)
    return jnp.where(mine, jnp.maximum(running, wide), running)


def blend_kernel(local, row_best, sib_rows, out):
    out[...] = jnp.maximum(jnp.maximum(local[...], row_best[0:blocks]), sib_rows[...])


def merge_kernel(plan, blended, back, out, best):
    rep = lax.axis_index("rep")
    best[...] = jnp.full((blocks, quarter), absent, jnp.float32)
    for number in range(len(every)):
        block = plan[at_back + number]
        best[pl.ds(block, 1), :] = jnp.maximum(
            best[pl.ds(block, 1), :], back[pl.ds(plan[at_back_row + number], 1), :]
        )
    merged = spread_in(blended[...], best[...], rep)
    lane = lax.broadcasted_iota(jnp.int32, (1, rows), 1)
    for b in range(blocks):
        out[b : b + 1, :] = jnp.where(lane < plan[at_own + b], merged[b : b + 1], -1.0)


def finish_kernel(one, two, out):
    best = jnp.maximum(one[...], two[...])
    for b in range(blocks):
        for q in range(n_rep):
            out[n_rep * b + q : n_rep * b + q + 1, :] = best[
                b : b + 1, q * quarter : (q + 1) * quarter
            ]


def higher_kernel(one, two, out):
    out[...] = jnp.maximum(one[...], two[...])


def move(value, dx, dz):
    if dx % n_x == 0 and dz % n_z == 0:
        return value
    steps = [
        (x * n_z + z, (x + dx) % n_x * n_z + (z + dz) % n_z) for x in range(n_x) for z in range(n_z)
    ]
    return lax.ppermute(value, ("x", "z"), steps)


def on_device(embeddings, valid_rows, pair_table):
    smem = pl.BlockSpec(memory_space=pltpu.SMEM)
    vmem = pl.BlockSpec(memory_space=pltpu.VMEM)
    hbm = pl.BlockSpec(memory_space=pl.ANY)
    pinned = pl.BlockSpec(memory_space=pltpu.HBM)
    params = pltpu.CompilerParams(vmem_limit_bytes=vmem_bytes)
    middle = pltpu.CompilerParams(vmem_limit_bytes=56 << 20)
    small = pltpu.CompilerParams(vmem_limit_bytes=8 << 20)
    cost = pl.CostEstimate(flops=0, bytes_accessed=1 << 16, transcendentals=0)
    f32, bf16 = jnp.float32, jnp.bfloat16
    part = (quarter, width)
    raw = embeddings.reshape(blocks, rows, width)

    def pick(wanted, spread, held, after, name):
        n = len(wanted)
        shapes = [(len(numbers),) + part for numbers in wanted]
        if spread:
            shapes = shapes[:-n_x] + [(n_x,) + shapes[-1]]
        return pl.pallas_call(
            functools.partial(pick_kernel, wanted, spread),
            out_shape=[jax.ShapeDtypeStruct(shape, bf16) for shape in shapes],
            in_specs=[smem] + [hbm] * len(held + after),
            out_specs=[hbm] * len(shapes),
            scratch_shapes=[
                pltpu.VMEM((n, 3) + part, bf16),
                pltpu.SemaphoreType.DMA((3 * n,)),
                pltpu.SemaphoreType.DMA((n,)),
            ],
            compiler_params=middle,
            cost_estimate=cost,
            name=name,
        )(plan, *held, *after)

    def compare(stage, feeds, arrays, past, after, name):
        slots = len(stages[stage])
        shapes = [(2 * blocks, rows), (slots, quarter)]
        if past:
            shapes = [(2 * blocks, rows), (2 * chips, quarter), (blocks, rows)]
        return pl.pallas_call(
            functools.partial(pair_kernel, stage, feeds),
            out_shape=[jax.ShapeDtypeStruct(shape, f32) for shape in shapes],
            in_specs=[smem, pinned] + [vmem] * len(past) + [hbm] * len(arrays + after),
            out_specs=[vmem] * len(shapes),
            scratch_shapes=[
                pltpu.VMEM((2 * blocks, rows, width), bf16),
                pltpu.VMEM((slots,) + part, bf16),
                pltpu.VMEM((slots // 8 * 8 + 8, quarter), f32),
                pltpu.SemaphoreType.DMA((2 * blocks,)),
                pltpu.SemaphoreType.DMA((len(feeds),)),
            ],
            compiler_params=middle,
            cost_estimate=cost,
            name=name,
        )(plan, units, *past, *arrays, *after)

    def numbers(wanted):
        return [[every.index(slot) for slot in slots] for slots in wanted]

    cols, *away, around = pl.pallas_call(
        prep_kernel,
        out_shape=[jax.ShapeDtypeStruct((blocks,) + part, bf16)]
        + [jax.ShapeDtypeStruct((1,) + part, bf16)] * n_x
        + [jax.ShapeDtypeStruct((2,) + part, bf16)],
        in_specs=[smem, hbm],
        out_specs=[hbm] * (2 + n_x),
        scratch_shapes=[
            pltpu.VMEM((blocks,) + part, bf16),
            pltpu.VMEM((blocks,) + part, bf16),
            pltpu.SemaphoreType.DMA((blocks,)),
            pltpu.SemaphoreType.DMA((len(far + down),)),
        ],
        compiler_params=params,
        cost_estimate=cost,
        name="prep",
    )(pair_table, raw)
    swap = [(0, 1), (1, 0)]
    sib_raw = lax.ppermute(raw, "core", swap)
    hop1 = move(cols, 0, 1)
    away = [move(a, dx, -2) for dx, a in enumerate(away)]
    plan = pl.pallas_call(
        plan_kernel,
        out_shape=jax.ShapeDtypeStruct((plan_size,), jnp.int32),
        in_specs=[smem, smem, hbm],
        out_specs=smem,
        scratch_shapes=[pltpu.SMEM((2 * blocks,), jnp.int32)],
        compiler_params=params,
        cost_estimate=cost,
        name="plan",
    )(pair_table, valid_rows, cols)
    units, local_best = pl.pallas_call(
        local_kernel,
        grid=(2 * blocks,),
        out_shape=(
            jax.ShapeDtypeStruct((2 * blocks, rows, width), bf16),
            jax.ShapeDtypeStruct((blocks, rows), f32),
        ),
        in_specs=[
            smem,
            pl.BlockSpec((1, rows, width), lambda i: (jnp.minimum(i, blocks - 1), 0, 0)),
            pl.BlockSpec((1, rows, width), lambda i: (jnp.maximum(i - blocks, 0), 0, 0)),
            pl.BlockSpec((blocks,) + part, lambda i: (0, 0, 0)),
        ],
        out_specs=(
            pl.BlockSpec((1, rows, width), lambda i: (i, 0, 0)),
            pl.BlockSpec((blocks, rows), lambda i: (0, 0)),
        ),
        compiler_params=params,
        cost_estimate=cost,
        name="local",
    )(valid_rows, raw, sib_raw, cols)
    hop1, away, local_best, plan = lax.optimization_barrier((hop1, away, local_best, plan))
    hop2 = move(hop1, 0, 1)
    away = move(jnp.concatenate(away, axis=0), 0, -2)
    picked = pick(numbers(first), False, [cols, hop1], [], "pick_a")
    first_in = [move(a, dx, 0) for dx, a in enumerate(picked)]
    hop2, away, around = lax.optimization_barrier((hop2, away, around))
    picked = pick(numbers(third + second), True, [cols, hop2], first_in, "pick_b")
    third_in = [move(a, slots[0][0], 1) for slots, a in zip(third, picked)]
    second_in = lax.all_to_all(picked[-1], "x", split_axis=0, concat_axis=0, tiled=True)
    down_in = move(around, 2, -3)

    past_a = compare(
        0,
        [(dx, None, 3, 3 * dx) for dx in range(n_x)] + [(n_x, None, n_x, 3 * n_x)],
        first_in + [away],
        [],
        [picked[0]],
        "pairs_a",
    )
    past_b = compare(
        1,
        [(0, None, 2, 0), (1, None, 2, 2)],
        third_in[:2],
        [],
        [past_a[0]],
        "pairs_b",
    )
    row_best, col_best, sib_best = compare(
        2,
        [(0, None, 2, 0), (1, None, 2, 2)] + [(2, dx, 2, 4 + 2 * dx) for dx in range(n_x)],
        [third_in[2], down_in, second_in],
        [*past_a, *past_b],
        [],
        "pairs_c",
    )
    sib_rows = lax.ppermute(sib_best, "core", swap)
    back = lax.all_to_all(col_best, ("x", "z"), split_axis=0, concat_axis=0, tiled=True)
    blended = pl.pallas_call(
        blend_kernel,
        out_shape=jax.ShapeDtypeStruct((blocks, rows), f32),
        in_specs=[vmem, vmem, vmem],
        out_specs=vmem,
        compiler_params=small,
        cost_estimate=cost,
        name="blend",
    )(local_best, row_best, sib_rows)
    combined = pl.pallas_call(
        merge_kernel,
        out_shape=jax.ShapeDtypeStruct((blocks, rows), f32),
        in_specs=[smem, vmem, vmem],
        out_specs=vmem,
        scratch_shapes=[pltpu.VMEM((blocks, quarter), f32)],
        compiler_params=small,
        cost_estimate=cost,
        name="merge",
    )(plan, blended, back)
    other = lax.ppermute(combined, "rep", [(y, y ^ 1) for y in range(n_rep)])
    combined = pl.pallas_call(
        higher_kernel,
        out_shape=jax.ShapeDtypeStruct((blocks, rows), f32),
        in_specs=[vmem, vmem],
        out_specs=vmem,
        compiler_params=small,
        cost_estimate=cost,
        name="higher",
    )(combined, other)
    other = lax.ppermute(combined, "rep", [(y, y ^ 2) for y in range(n_rep)])
    result = pl.pallas_call(
        finish_kernel,
        out_shape=jax.ShapeDtypeStruct((blocks * n_rep, quarter), f32),
        in_specs=[vmem, vmem],
        out_specs=vmem,
        compiler_params=small,
        cost_estimate=cost,
        name="finish",
    )(combined, other)
    return result.reshape(-1)


def solution(mesh):
    grid = Mesh(mesh.devices.reshape(n_x, n_z, n_core, n_rep), ("x", "z", "core", "rep"))
    return jax.shard_map(
        on_device,
        mesh=grid,
        in_specs=(P(("x", "z", "core"), None), P(), P()),
        out_specs=P(("x", "z", "core")),
        check_vma=False,
    )
```

```python
import functools

import jax
import jax.numpy as jnp
from jax import lax
from jax.experimental import pallas as pl
from jax.experimental.pallas import tpu as pltpu
from jax.sharding import Mesh, PartitionSpec as P

absent = -2.0
epsilon = 1e-06
n_x, n_z, n_core, n_rep = 4, 8, 2, 4
chips = n_x * n_z
blocks = 8
rows = 512
quarter = rows // n_rep
width = 768
vmem_bytes = 60 << 20


def dot_t(left, right):
    return lax.dot_general(
        left, right, (((1,), (1,)), ((), ())), preferred_element_type=jnp.float32
    )


def normalise(raw):
    wide = raw.astype(jnp.float32)
    scale = lax.rsqrt(jnp.sum(wide * wide, axis=-1, keepdims=True) + epsilon)
    return (wide * scale).astype(jnp.bfloat16)


def place():
    return lax.axis_index("x"), lax.axis_index("z"), lax.axis_index("core"), lax.axis_index("rep")


def pair_info(table, source, target, core, many, which):
    side = which if many == 2 else jnp.where(source < target, core, 1 - core)
    forth = table[source * n_core + core, target * n_core + side]
    back = table[target * n_core + side, source * n_core + core]
    live = (forth >= 0) | (back >= 0)
    if many == 1:
        live = live & ((source != target) | (core == 0))
    source_block = jnp.where(forth >= 0, forth >> 3, back & 7)
    target_block = jnp.where(forth >= 0, forth & 7, (back >> 3) & 7)
    return live, side, source_block, target_block


def chip_at(x, z, dx, dz):
    return ((x + dx + n_x) & (n_x - 1)) * n_z + ((z + dz + n_z) & (n_z - 1))


first = [[(dx, 0, 1, 0), (dx, 1, 2, 0), (dx, 1, 2, 1)] for dx in range(n_x)]
second = [[(dx, 2, 2, 0), (dx, 2, 2, 1)] for dx in range(n_x)]
third = [[(dx, 3, 2, 0), (dx, 3, 2, 1)] for dx in (0, 1, 3)]
far = [(dx, 4, 1, 0) for dx in range(n_x)]
down = [(2, 5, 2, 0), (2, 5, 2, 1)]
stages = [sum(first, []) + far, third[0] + third[1], third[2] + down + sum(second, [])]
every = sum(stages, [])
gone_of = {0: 0, 1: 1, 2: 2, 3: 2}
at_pick, at_back, at_back_row, at_row, at_own = 0, 32, 64, 96, 128
at_stage, plan_size = [], 144
for stage in stages:
    at_stage.append(plan_size)
    plan_size += 16 + len(stage) + 1 + 1 + 3 * (len(stage) + 2)


def places(stage, base):
    slots = len(stage)
    counts = base + 2 * blocks
    groups = counts + slots + 1
    own_of = groups + 1
    return counts, groups, own_of, own_of + slots + 2, own_of + 2 * (slots + 2)


def plan_kernel(table, valid, after, plan, latest):
    x, z, core, rep = place()
    chip = chip_at(x, z, 0, 0)
    start = rep * quarter
    for o in range(2 * blocks):
        owner = chip * n_core + (core if o < blocks else 1 - core)
        plan[at_own + o] = valid[owner * blocks + o % blocks]
    number = 0
    for stage, base in zip(stages, at_stage):
        slots = len(stage)
        counts, groups, own_of, first_of, second_of = places(stage, base)
        for o in range(2 * blocks):
            plan[base + o] = 0
            latest[o] = 0
        plan[groups] = 0
        for slot, (dx, dz, many, which) in enumerate(stage):
            target = chip_at(x, z, dx, dz)
            _, _, block, _ = pair_info(table, chip, target, core, many, which)
            plan[at_back + number] = block
            plan[at_back_row + number] = 2 * target + which
            if dz in gone_of:
                gone = gone_of[dz]
                source, target = chip_at(x, z, 0, -gone), chip_at(x, z, dx, dz - gone)
                _, _, block, _ = pair_info(table, source, target, core, many, which)
                plan[at_pick + number] = block
            source = chip_at(x, z, -dx, -dz)
            live, side, block, own_block = pair_info(table, source, chip, core, many, which)
            mine = jnp.where(side == core, 0, blocks) + own_block
            count = plan[groups]
            joins = (plan[base + mine] & 1) == 1
            group = jnp.where(live, jnp.where(joins, latest[mine], count), slots + 1)
            plan[own_of + group] = mine
            plan[first_of + group] = jnp.where(joins, plan[first_of + group], slot)
            plan[second_of + group] = jnp.where(joins, slot, slots)
            latest[mine] = jnp.where(live, group, latest[mine])
            plan[groups] = count + (live & jnp.logical_not(joins)).astype(jnp.int32)
            plan[base + mine] = plan[base + mine] + live.astype(jnp.int32)
            plan[counts + slot] = valid[(source * n_core + core) * blocks + block] - start
            plan[at_row + number] = 2 * source + which
            number += 1
        plan[counts + slots] = 0
        count = plan[groups]
        plan[own_of + count] = plan[own_of]
        plan[first_of + count] = slots
        plan[second_of + count] = slots


def prep_kernel(table, emb, units, to0, to1, to2, to3, around, raw, unit, sem_in, sems):
    x, z, core, rep = place()
    chip = chip_at(x, z, 0, 0)
    loads = [
        pltpu.make_async_copy(emb.at[b, pl.ds(rep * quarter, quarter)], raw.at[b], sem_in.at[b])
        for b in range(blocks)
    ]
    for load in loads:
        load.start()
    copies = []
    for b in range(blocks):
        loads[b].wait()
        unit[b] = normalise(raw[b])
        copies.append(pltpu.make_async_copy(unit.at[b], units.at[b], sem_in.at[b]))
        copies[-1].start()
    outs = [to0.at[0], to1.at[0], to2.at[0], to3.at[0], around.at[0], around.at[1]]
    for a, (dx, dz, many, which) in enumerate(far + down):
        _, _, block, _ = pair_info(table, chip, chip_at(x, z, dx, dz), core, many, which)
        copies.append(pltpu.make_async_copy(unit.at[block], outs[a], sems.at[a]))
        copies[-1].start()
    for copy in copies:
        copy.wait()


def pick_kernel(wanted, spread, plan, *refs):
    near_by, hop = refs[:2]
    parts, get_sems, put_sems = refs[-3:]
    x, z, core, rep = place()
    n = len(wanted)
    if spread:
        outs = list(refs[-n + n_x - 4 : -4])
        outs += [refs[-4].at[(x + dx) & (n_x - 1)] for dx in range(n_x)]
    else:
        outs = refs[-n - 3 : -3]
    gets, puts = [], []
    for a, numbers in enumerate(wanted):
        for place_in, number in enumerate(numbers):
            held = near_by if every[number][1] == 0 else hop
            gets.append(
                pltpu.make_async_copy(
                    held.at[plan[at_pick + number]],
                    parts.at[a, place_in],
                    get_sems.at[3 * a + place_in],
                )
            )
            gets[-1].start()
    left = list(gets)
    for a, (out, numbers) in enumerate(zip(outs, wanted)):
        for _ in numbers:
            left.pop(0).wait()
        puts.append(
            pltpu.make_async_copy(parts.at[a, pl.ds(0, len(numbers))], out, put_sems.at[a])
        )
        puts[-1].start()
    for copy in puts:
        copy.wait()


def local_kernel(valid, own, sib, cols, unit_out, best):
    step = pl.program_id(0)
    x, z, core, rep = place()
    dev = chip_at(x, z, 0, 0) * n_core + core
    start = rep * quarter

    @pl.when(step >= blocks)
    def _():
        unit_out[0] = normalise(sib[0])

    @pl.when(step < blocks)
    def _():
        mine = normalise(own[0])
        unit_out[0] = mine
        part = lax.broadcasted_iota(jnp.int32, (quarter, rows), 0)
        gap = lax.broadcasted_iota(jnp.int32, (quarter, rows), 1) - part
        found = jnp.full((1, rows), absent, jnp.float32)
        for k in range(0, blocks, 2):
            pair = jnp.concatenate([cols[k], cols[k + 1]], axis=0)
            scores = dot_t(pair, mine)
            for half in range(2):
                count = valid[dev * blocks + k + half] - start
                own_gap = jnp.where(k + half == step, start, rows)
                allowed = (part < count) & (gap != own_gap)
                here = jnp.where(allowed, scores[half * quarter : (half + 1) * quarter], absent)
                found = jnp.maximum(found, jnp.max(here, axis=0, keepdims=True))
        best[pl.ds(step, 1), :] = found


def pair_kernel(stage, feeds, plan, own, *refs):
    final = stage == len(stages) - 1
    slots, base = len(stages[stage]), at_stage[stage]
    counts, groups, own_of, first_of, second_of = places(stages[stage], base)
    units, held, cols, sem_u, sem_g = refs[-5:]
    outs, arrays, past = refs[-8 if final else -7 : -5], refs, ()
    if final:
        past, arrays = refs[: 2 * stage], refs[2 * stage :]
    x, z, core, rep = place()
    gets = []
    for a, (array, dx, count, first_slot) in enumerate(feeds):
        came = arrays[array] if dx is None else arrays[array].at[(x - dx + n_x) & (n_x - 1)]
        gets.append(pltpu.make_async_copy(came, held.at[pl.ds(first_slot, count)], sem_g.at[a]))
        gets[-1].start()
    loads = []
    for o in range(2 * blocks):
        loads.append(pltpu.make_async_copy(own.at[o], units.at[o], sem_u.at[o]))

        @pl.when(plan[base + o] > 0)
        def _():
            loads[o].start()

    row_out, col_out = outs[:2]
    row_out[...] = jnp.full((2 * blocks, rows), absent, jnp.float32)
    for ref in past[::2]:
        row_out[...] = jnp.maximum(row_out[...], ref[...])
    cols[...] = jnp.full(cols.shape, absent, jnp.float32)
    if final:
        col_out[...] = jnp.full(col_out.shape, absent, jnp.float32)
        number = 0
        for ref, done in zip(past[1::2], stages):
            for slot in range(len(done)):
                col_out[pl.ds(plan[at_row + number], 1), :] = ref[slot : slot + 1, :]
                number += 1
    part = lax.broadcasted_iota(jnp.int32, (quarter, rows), 0)
    lane = lax.broadcasted_iota(jnp.int32, (2 * quarter, rows), 1)
    for copy in gets:
        copy.wait()
    for o in range(2 * blocks):

        @pl.when(plan[base + o] > 0)
        def _():
            loads[o].wait()

    def visit(turn, carry):
        for group in (2 * turn, 2 * turn + 1):
            o = plan[own_of + group]
            pair = [plan[first_of + group], plan[second_of + group]]
            here_slot = [jnp.minimum(slot, slots - 1) for slot in pair]
            scores = dot_t(
                jnp.concatenate([held[here_slot[0]], held[here_slot[1]]], axis=0), units[o]
            )
            ok = jnp.where(lane < plan[at_own + o], scores, absent)
            folded = jnp.maximum(
                jnp.maximum(ok[:, 0:128], ok[:, 128:256]), jnp.maximum(ok[:, 256:384], ok[:, 384:512])
            )
            top = jnp.full((1, rows), absent, jnp.float32)
            for half in range(2):
                span = slice(half * quarter, (half + 1) * quarter)
                here = jnp.where(part < plan[counts + pair[half]], scores[span], absent)
                top = jnp.maximum(top, jnp.max(here, axis=0, keepdims=True))
                cols[pl.ds(pair[half], 1), :] = jnp.max(folded[span].T, axis=0, keepdims=True)
            row_out[pl.ds(o, 1), :] = jnp.maximum(row_out[pl.ds(o, 1), :], top)
        return carry

    lax.fori_loop(0, (plan[groups] + 1) >> 1, visit, 0)
    if final:
        outs[2][...] = row_out[blocks:]
        for slot in range(slots):
            number = len(every) - slots + slot
            col_out[pl.ds(plan[at_row + number], 1), :] = cols[slot : slot + 1, :]
    else:
        col_out[...] = cols[0:slots]


def spread_in(running, best, rep):
    wide = jnp.concatenate([best] * n_rep, axis=1)
    lane = lax.broadcasted_iota(jnp.int32, (blocks, rows), 1)
    mine = (lane >= rep * quarter) & (lane < (rep + 1) * quarter)
    return jnp.where(mine, jnp.maximum(running, wide), running)


def blend_kernel(local, row_best, sib_rows, out):
    out[...] = jnp.maximum(jnp.maximum(local[...], row_best[0:blocks]), sib_rows[...])


def merge_kernel(plan, blended, back, out, best):
    rep = lax.axis_index("rep")
    best[...] = jnp.full((blocks, quarter), absent, jnp.float32)
    for number in range(len(every)):
        block = plan[at_back + number]
        best[pl.ds(block, 1), :] = jnp.maximum(
            best[pl.ds(block, 1), :], back[pl.ds(plan[at_back_row + number], 1), :]
        )
    merged = spread_in(blended[...], best[...], rep)
    lane = lax.broadcasted_iota(jnp.int32, (1, rows), 1)
    for b in range(blocks):
        out[b : b + 1, :] = jnp.where(lane < plan[at_own + b], merged[b : b + 1], -1.0)


def finish_kernel(one, two, three, four, out):
    best = jnp.maximum(jnp.maximum(one[...], two[...]), jnp.maximum(three[...], four[...]))
    for b in range(blocks):
        for q in range(n_rep):
            out[n_rep * b + q : n_rep * b + q + 1, :] = best[
                b : b + 1, q * quarter : (q + 1) * quarter
            ]


def move(value, dx, dz):
    if dx % n_x == 0 and dz % n_z == 0:
        return value
    steps = [
        (x * n_z + z, (x + dx) % n_x * n_z + (z + dz) % n_z) for x in range(n_x) for z in range(n_z)
    ]
    return lax.ppermute(value, ("x", "z"), steps)


def on_device(embeddings, valid_rows, pair_table):
    smem = pl.BlockSpec(memory_space=pltpu.SMEM)
    vmem = pl.BlockSpec(memory_space=pltpu.VMEM)
    hbm = pl.BlockSpec(memory_space=pl.ANY)
    pinned = pl.BlockSpec(memory_space=pltpu.HBM)
    params = pltpu.CompilerParams(vmem_limit_bytes=vmem_bytes)
    middle = pltpu.CompilerParams(vmem_limit_bytes=56 << 20)
    small = pltpu.CompilerParams(vmem_limit_bytes=8 << 20)
    cost = pl.CostEstimate(flops=0, bytes_accessed=1 << 16, transcendentals=0)
    f32, bf16 = jnp.float32, jnp.bfloat16
    part = (quarter, width)
    raw = embeddings.reshape(blocks, rows, width)

    def pick(wanted, spread, held, after, name):
        n = len(wanted)
        shapes = [(len(numbers),) + part for numbers in wanted]
        if spread:
            shapes = shapes[:-n_x] + [(n_x,) + shapes[-1]]
        return pl.pallas_call(
            functools.partial(pick_kernel, wanted, spread),
            out_shape=[jax.ShapeDtypeStruct(shape, bf16) for shape in shapes],
            in_specs=[smem] + [hbm] * len(held + after),
            out_specs=[hbm] * len(shapes),
            scratch_shapes=[
                pltpu.VMEM((n, 3) + part, bf16),
                pltpu.SemaphoreType.DMA((3 * n,)),
                pltpu.SemaphoreType.DMA((n,)),
            ],
            compiler_params=middle,
            cost_estimate=cost,
            name=name,
        )(plan, *held, *after)

    def compare(stage, feeds, arrays, past, after, name):
        slots = len(stages[stage])
        shapes = [(2 * blocks, rows), (slots, quarter)]
        if past:
            shapes = [(2 * blocks, rows), (2 * chips, quarter), (blocks, rows)]
        return pl.pallas_call(
            functools.partial(pair_kernel, stage, feeds),
            out_shape=[jax.ShapeDtypeStruct(shape, f32) for shape in shapes],
            in_specs=[smem, pinned] + [vmem] * len(past) + [hbm] * len(arrays + after),
            out_specs=[vmem] * len(shapes),
            scratch_shapes=[
                pltpu.VMEM((2 * blocks, rows, width), bf16),
                pltpu.VMEM((slots,) + part, bf16),
                pltpu.VMEM((slots // 8 * 8 + 8, quarter), f32),
                pltpu.SemaphoreType.DMA((2 * blocks,)),
                pltpu.SemaphoreType.DMA((len(feeds),)),
            ],
            compiler_params=middle,
            cost_estimate=cost,
            name=name,
        )(plan, units, *past, *arrays, *after)

    def numbers(wanted):
        return [[every.index(slot) for slot in slots] for slots in wanted]

    cols, *away, around = pl.pallas_call(
        prep_kernel,
        out_shape=[jax.ShapeDtypeStruct((blocks,) + part, bf16)]
        + [jax.ShapeDtypeStruct((1,) + part, bf16)] * n_x
        + [jax.ShapeDtypeStruct((2,) + part, bf16)],
        in_specs=[smem, hbm],
        out_specs=[hbm] * (2 + n_x),
        scratch_shapes=[
            pltpu.VMEM((blocks,) + part, bf16),
            pltpu.VMEM((blocks,) + part, bf16),
            pltpu.SemaphoreType.DMA((blocks,)),
            pltpu.SemaphoreType.DMA((len(far + down),)),
        ],
        compiler_params=params,
        cost_estimate=cost,
        name="prep",
    )(pair_table, raw)
    swap = [(0, 1), (1, 0)]
    sib_raw = lax.ppermute(raw, "core", swap)
    hop1 = move(cols, 0, 1)
    away = [move(a, dx, -2) for dx, a in enumerate(away)]
    plan = pl.pallas_call(
        plan_kernel,
        out_shape=jax.ShapeDtypeStruct((plan_size,), jnp.int32),
        in_specs=[smem, smem, hbm],
        out_specs=smem,
        scratch_shapes=[pltpu.SMEM((2 * blocks,), jnp.int32)],
        compiler_params=params,
        cost_estimate=cost,
        name="plan",
    )(pair_table, valid_rows, cols)
    units, local_best = pl.pallas_call(
        local_kernel,
        grid=(2 * blocks,),
        out_shape=(
            jax.ShapeDtypeStruct((2 * blocks, rows, width), bf16),
            jax.ShapeDtypeStruct((blocks, rows), f32),
        ),
        in_specs=[
            smem,
            pl.BlockSpec((1, rows, width), lambda i: (jnp.minimum(i, blocks - 1), 0, 0)),
            pl.BlockSpec((1, rows, width), lambda i: (jnp.maximum(i - blocks, 0), 0, 0)),
            pl.BlockSpec((blocks,) + part, lambda i: (0, 0, 0)),
        ],
        out_specs=(
            pl.BlockSpec((1, rows, width), lambda i: (i, 0, 0)),
            pl.BlockSpec((blocks, rows), lambda i: (0, 0)),
        ),
        compiler_params=params,
        cost_estimate=cost,
        name="local",
    )(valid_rows, raw, sib_raw, cols)
    hop1, away, local_best, plan = lax.optimization_barrier((hop1, away, local_best, plan))
    hop2 = move(hop1, 0, 1)
    away = move(jnp.concatenate(away, axis=0), 0, -2)
    picked = pick(numbers(first), False, [cols, hop1], [], "pick_a")
    first_in = [move(a, dx, 0) for dx, a in enumerate(picked)]
    hop2, away, around, *first_in = lax.optimization_barrier((hop2, away, around, *first_in))
    picked = pick(numbers(third + second), True, [cols, hop2], [], "pick_b")
    third_in = [move(a, slots[0][0], 1) for slots, a in zip(third, picked)]
    second_in = lax.all_to_all(picked[-1], "x", split_axis=0, concat_axis=0, tiled=True)
    down_in = move(around, 2, -3)

    past_a = compare(
        0,
        [(dx, None, 3, 3 * dx) for dx in range(n_x)] + [(n_x, None, n_x, 3 * n_x)],
        first_in + [away],
        [],
        [picked[0]],
        "pairs_a",
    )
    past_b = compare(
        1,
        [(0, None, 2, 0), (1, None, 2, 2)],
        third_in[:2],
        [],
        [past_a[0]],
        "pairs_b",
    )
    row_best, col_best, sib_best = compare(
        2,
        [(0, None, 2, 0), (1, None, 2, 2)] + [(2, dx, 2, 4 + 2 * dx) for dx in range(n_x)],
        [third_in[2], down_in, second_in],
        [*past_a, *past_b],
        [],
        "pairs_c",
    )
    sib_rows = lax.ppermute(sib_best, "core", swap)
    back = lax.all_to_all(col_best, ("x", "z"), split_axis=0, concat_axis=0, tiled=True)
    blended = pl.pallas_call(
        blend_kernel,
        out_shape=jax.ShapeDtypeStruct((blocks, rows), f32),
        in_specs=[vmem, vmem, vmem],
        out_specs=vmem,
        compiler_params=small,
        cost_estimate=cost,
        name="blend",
    )(local_best, row_best, sib_rows)
    combined = pl.pallas_call(
        merge_kernel,
        out_shape=jax.ShapeDtypeStruct((blocks, rows), f32),
        in_specs=[smem, vmem, vmem],
        out_specs=vmem,
        scratch_shapes=[pltpu.VMEM((blocks, quarter), f32)],
        compiler_params=small,
        cost_estimate=cost,
        name="merge",
    )(plan, blended, back)
    others = [
        lax.ppermute(combined, "rep", [(y, (y + d) % n_rep) for y in range(n_rep)])
        for d in range(1, n_rep)
    ]
    result = pl.pallas_call(
        finish_kernel,
        out_shape=jax.ShapeDtypeStruct((blocks * n_rep, quarter), f32),
        in_specs=[vmem, vmem, vmem, vmem],
        out_specs=vmem,
        compiler_params=small,
        cost_estimate=cost,
        name="finish",
    )(combined, *others)
    return result.reshape(-1)


def solution(mesh):
    grid = Mesh(mesh.devices.reshape(n_x, n_z, n_core, n_rep), ("x", "z", "core", "rep"))
    return jax.shard_map(
        on_device,
        mesh=grid,
        in_specs=(P(("x", "z", "core"), None), P(), P()),
        out_specs=P(("x", "z", "core")),
        check_vma=False,
    )
```

```python
import functools

import jax
import jax.numpy as jnp
from jax import lax
from jax.experimental import pallas as pl
from jax.experimental.pallas import tpu as pltpu
from jax.sharding import Mesh, PartitionSpec as P

absent = -2.0
epsilon = 1e-06
n_x, n_z, n_core, n_rep = 4, 8, 2, 4
chips = n_x * n_z
blocks = 8
rows = 512
quarter = rows // n_rep
width = 768
vmem_bytes = 60 << 20


def dot_t(left, right):
    return lax.dot_general(
        left, right, (((1,), (1,)), ((), ())), preferred_element_type=jnp.float32
    )


def normalise(raw):
    wide = raw.astype(jnp.float32)
    scale = lax.rsqrt(jnp.sum(wide * wide, axis=-1, keepdims=True) + epsilon)
    return (wide * scale).astype(jnp.bfloat16)


def place():
    return lax.axis_index("x"), lax.axis_index("z"), lax.axis_index("core"), lax.axis_index("rep")


def pair_info(table, source, target, core, many, which):
    side = which if many == 2 else jnp.where(source < target, core, 1 - core)
    forth = table[source * n_core + core, target * n_core + side]
    back = table[target * n_core + side, source * n_core + core]
    live = (forth >= 0) | (back >= 0)
    if many == 1:
        live = live & ((source != target) | (core == 0))
    source_block = jnp.where(forth >= 0, forth >> 3, back & 7)
    target_block = jnp.where(forth >= 0, forth & 7, (back >> 3) & 7)
    return live, side, source_block, target_block


def chip_at(x, z, dx, dz):
    return ((x + dx + n_x) & (n_x - 1)) * n_z + ((z + dz + n_z) & (n_z - 1))


first = [[(dx, 0, 1, 0), (dx, 1, 2, 0), (dx, 1, 2, 1)] for dx in range(n_x)]
second = [[(dx, 2, 2, 0), (dx, 2, 2, 1)] for dx in range(n_x)]
third = [[(dx, 3, 2, 0), (dx, 3, 2, 1)] for dx in (0, 1, 3)]
far = [(dx, 4, 1, 0) for dx in range(n_x)]
extra, down = [(2, 3, 1, 0)], [(2, 5, 1, 0)]
stages = [sum(first, []) + far, third[0] + third[1], third[2] + extra + down + sum(second, [])]
every = sum(stages, [])
gone_of = {0: 0, 1: 1, 2: 2, 3: 2, 5: 0}
at_pick, at_back, at_back_row, at_row, at_own = 0, 32, 64, 96, 128
at_stage, plan_size = [], 144
for stage in stages:
    at_stage.append(plan_size)
    plan_size += 16 + len(stage) + 1 + 1 + 3 * (len(stage) + 2)


def places(stage, base):
    slots = len(stage)
    counts = base + 2 * blocks
    groups = counts + slots + 1
    own_of = groups + 1
    return counts, groups, own_of, own_of + slots + 2, own_of + 2 * (slots + 2)


def plan_kernel(table, valid, after, plan, latest):
    x, z, core, rep = place()
    chip = chip_at(x, z, 0, 0)
    start = rep * quarter
    for o in range(2 * blocks):
        owner = chip * n_core + (core if o < blocks else 1 - core)
        plan[at_own + o] = valid[owner * blocks + o % blocks]
    number = 0
    for stage, base in zip(stages, at_stage):
        slots = len(stage)
        counts, groups, own_of, first_of, second_of = places(stage, base)
        for o in range(2 * blocks):
            plan[base + o] = 0
            latest[o] = 0
        plan[groups] = 0
        for slot, (dx, dz, many, which) in enumerate(stage):
            target = chip_at(x, z, dx, dz)
            _, _, block, _ = pair_info(table, chip, target, core, many, which)
            plan[at_back + number] = block
            plan[at_back_row + number] = 2 * target + which
            if dz in gone_of:
                gone = gone_of[dz]
                source, target = chip_at(x, z, 0, -gone), chip_at(x, z, dx, dz - gone)
                _, _, block, _ = pair_info(table, source, target, core, many, which)
                plan[at_pick + number] = block
            source = chip_at(x, z, -dx, -dz)
            live, side, block, own_block = pair_info(table, source, chip, core, many, which)
            mine = jnp.where(side == core, 0, blocks) + own_block
            count = plan[groups]
            joins = (plan[base + mine] & 1) == 1
            group = jnp.where(live, jnp.where(joins, latest[mine], count), slots + 1)
            plan[own_of + group] = mine
            plan[first_of + group] = jnp.where(joins, plan[first_of + group], slot)
            plan[second_of + group] = jnp.where(joins, slot, slots)
            latest[mine] = jnp.where(live, group, latest[mine])
            plan[groups] = count + (live & jnp.logical_not(joins)).astype(jnp.int32)
            plan[base + mine] = plan[base + mine] + live.astype(jnp.int32)
            plan[counts + slot] = valid[(source * n_core + core) * blocks + block] - start
            plan[at_row + number] = 2 * source + which
            number += 1
        plan[counts + slots] = 0
        count = plan[groups]
        plan[own_of + count] = plan[own_of]
        plan[first_of + count] = slots
        plan[second_of + count] = slots


def prep_kernel(table, emb, units, to0, to1, to2, to3, raw, unit, sem_in, sems):
    x, z, core, rep = place()
    chip = chip_at(x, z, 0, 0)
    loads = [
        pltpu.make_async_copy(emb.at[b, pl.ds(rep * quarter, quarter)], raw.at[b], sem_in.at[b])
        for b in range(blocks)
    ]
    for load in loads:
        load.start()
    copies = []
    for b in range(blocks):
        loads[b].wait()
        unit[b] = normalise(raw[b])
        copies.append(pltpu.make_async_copy(unit.at[b], units.at[b], sem_in.at[b]))
        copies[-1].start()
    outs = [to0.at[0], to1.at[0], to2.at[0], to3.at[0]]
    for a, (dx, dz, many, which) in enumerate(far):
        _, _, block, _ = pair_info(table, chip, chip_at(x, z, dx, dz), core, many, which)
        copies.append(pltpu.make_async_copy(unit.at[block], outs[a], sems.at[a]))
        copies[-1].start()
    for copy in copies:
        copy.wait()


def pick_kernel(wanted, spread, plan, *refs):
    near_by, hop = refs[:2]
    parts, get_sems, put_sems = refs[-3:]
    x, z, core, rep = place()
    n = len(wanted)
    if spread:
        outs = list(refs[-n + n_x - 4 : -4])
        outs += [refs[-4].at[(x + dx) & (n_x - 1)] for dx in range(n_x)]
    else:
        outs = refs[-n - 3 : -3]
    gets, puts = [], []
    for a, numbers in enumerate(wanted):
        for place_in, number in enumerate(numbers):
            held = near_by if every[number][1] in (0, 5) else hop
            gets.append(
                pltpu.make_async_copy(
                    held.at[plan[at_pick + number]],
                    parts.at[a, place_in],
                    get_sems.at[4 * a + place_in],
                )
            )
            gets[-1].start()
    left = list(gets)
    for a, (out, numbers) in enumerate(zip(outs, wanted)):
        for _ in numbers:
            left.pop(0).wait()
        puts.append(
            pltpu.make_async_copy(parts.at[a, pl.ds(0, len(numbers))], out, put_sems.at[a])
        )
        puts[-1].start()
    for copy in puts:
        copy.wait()


def local_kernel(valid, own, sib, cols, unit_out, best):
    step = pl.program_id(0)
    x, z, core, rep = place()
    dev = chip_at(x, z, 0, 0) * n_core + core
    start = rep * quarter

    @pl.when(step >= blocks)
    def _():
        unit_out[0] = normalise(sib[0])

    @pl.when(step < blocks)
    def _():
        mine = normalise(own[0])
        unit_out[0] = mine
        part = lax.broadcasted_iota(jnp.int32, (quarter, rows), 0)
        gap = lax.broadcasted_iota(jnp.int32, (quarter, rows), 1) - part
        found = jnp.full((1, rows), absent, jnp.float32)
        for k in range(0, blocks, 2):
            pair = jnp.concatenate([cols[k], cols[k + 1]], axis=0)
            scores = dot_t(pair, mine)
            for half in range(2):
                count = valid[dev * blocks + k + half] - start
                own_gap = jnp.where(k + half == step, start, rows)
                allowed = (part < count) & (gap != own_gap)
                here = jnp.where(allowed, scores[half * quarter : (half + 1) * quarter], absent)
                found = jnp.maximum(found, jnp.max(here, axis=0, keepdims=True))
        best[pl.ds(step, 1), :] = found


def pair_kernel(stage, feeds, plan, own, *refs):
    final = stage == len(stages) - 1
    slots, base = len(stages[stage]), at_stage[stage]
    counts, groups, own_of, first_of, second_of = places(stages[stage], base)
    units, held, cols, sem_u, sem_g = refs[-5:]
    outs, arrays, past = refs[-8 if final else -7 : -5], refs, ()
    if final:
        past, arrays = refs[: 2 * stage], refs[2 * stage :]
    x, z, core, rep = place()
    gets = []
    for a, (array, dx, count, first_slot) in enumerate(feeds):
        came = arrays[array].at[pl.ds(0, count)]
        if dx is not None:
            came = arrays[array].at[(x - dx + n_x) & (n_x - 1)]
        gets.append(pltpu.make_async_copy(came, held.at[pl.ds(first_slot, count)], sem_g.at[a]))
        gets[-1].start()
    loads = []
    for o in range(2 * blocks):
        loads.append(pltpu.make_async_copy(own.at[o], units.at[o], sem_u.at[o]))

        @pl.when(plan[base + o] > 0)
        def _():
            loads[o].start()

    row_out, col_out = outs[:2]
    row_out[...] = jnp.full((2 * blocks, rows), absent, jnp.float32)
    for ref in past[::2]:
        row_out[...] = jnp.maximum(row_out[...], ref[...])
    cols[...] = jnp.full(cols.shape, absent, jnp.float32)
    if final:
        col_out[...] = jnp.full(col_out.shape, absent, jnp.float32)
        number = 0
        for ref, done in zip(past[1::2], stages):
            for slot in range(len(done)):
                col_out[pl.ds(plan[at_row + number], 1), :] = ref[slot : slot + 1, :]
                number += 1
    part = lax.broadcasted_iota(jnp.int32, (quarter, rows), 0)
    lane = lax.broadcasted_iota(jnp.int32, (2 * quarter, rows), 1)
    for copy in gets:
        copy.wait()
    for o in range(2 * blocks):

        @pl.when(plan[base + o] > 0)
        def _():
            loads[o].wait()

    def visit(turn, carry):
        for group in (2 * turn, 2 * turn + 1):
            o = plan[own_of + group]
            pair = [plan[first_of + group], plan[second_of + group]]
            here_slot = [jnp.minimum(slot, slots - 1) for slot in pair]
            scores = dot_t(
                jnp.concatenate([held[here_slot[0]], held[here_slot[1]]], axis=0), units[o]
            )
            ok = jnp.where(lane < plan[at_own + o], scores, absent)
            folded = jnp.maximum(
                jnp.maximum(ok[:, 0:128], ok[:, 128:256]), jnp.maximum(ok[:, 256:384], ok[:, 384:512])
            )
            top = jnp.full((1, rows), absent, jnp.float32)
            for half in range(2):
                span = slice(half * quarter, (half + 1) * quarter)
                here = jnp.where(part < plan[counts + pair[half]], scores[span], absent)
                top = jnp.maximum(top, jnp.max(here, axis=0, keepdims=True))
                cols[pl.ds(pair[half], 1), :] = jnp.max(folded[span].T, axis=0, keepdims=True)
            row_out[pl.ds(o, 1), :] = jnp.maximum(row_out[pl.ds(o, 1), :], top)
        return carry

    lax.fori_loop(0, (plan[groups] + 1) >> 1, visit, 0)
    if final:
        outs[2][...] = row_out[blocks:]
        for slot in range(slots):
            number = len(every) - slots + slot
            col_out[pl.ds(plan[at_row + number], 1), :] = cols[slot : slot + 1, :]
    else:
        col_out[...] = cols[0:slots]


def spread_in(running, best, rep):
    wide = jnp.concatenate([best] * n_rep, axis=1)
    lane = lax.broadcasted_iota(jnp.int32, (blocks, rows), 1)
    mine = (lane >= rep * quarter) & (lane < (rep + 1) * quarter)
    return jnp.where(mine, jnp.maximum(running, wide), running)


def blend_kernel(local, row_best, sib_rows, out):
    out[...] = jnp.maximum(jnp.maximum(local[...], row_best[0:blocks]), sib_rows[...])


def merge_kernel(plan, blended, back, out, best):
    rep = lax.axis_index("rep")
    best[...] = jnp.full((blocks, quarter), absent, jnp.float32)
    for number in range(len(every)):
        block = plan[at_back + number]
        best[pl.ds(block, 1), :] = jnp.maximum(
            best[pl.ds(block, 1), :], back[pl.ds(plan[at_back_row + number], 1), :]
        )
    merged = spread_in(blended[...], best[...], rep)
    lane = lax.broadcasted_iota(jnp.int32, (1, rows), 1)
    for b in range(blocks):
        out[b : b + 1, :] = jnp.where(lane < plan[at_own + b], merged[b : b + 1], -1.0)


def finish_kernel(one, two, three, four, out):
    best = jnp.maximum(jnp.maximum(one[...], two[...]), jnp.maximum(three[...], four[...]))
    for b in range(blocks):
        for q in range(n_rep):
            out[n_rep * b + q : n_rep * b + q + 1, :] = best[
                b : b + 1, q * quarter : (q + 1) * quarter
            ]


def move(value, dx, dz):
    if dx % n_x == 0 and dz % n_z == 0:
        return value
    steps = [
        (x * n_z + z, (x + dx) % n_x * n_z + (z + dz) % n_z) for x in range(n_x) for z in range(n_z)
    ]
    return lax.ppermute(value, ("x", "z"), steps)


def on_device(embeddings, valid_rows, pair_table):
    smem = pl.BlockSpec(memory_space=pltpu.SMEM)
    vmem = pl.BlockSpec(memory_space=pltpu.VMEM)
    hbm = pl.BlockSpec(memory_space=pl.ANY)
    pinned = pl.BlockSpec(memory_space=pltpu.HBM)
    params = pltpu.CompilerParams(vmem_limit_bytes=vmem_bytes)
    middle = pltpu.CompilerParams(vmem_limit_bytes=56 << 20)
    small = pltpu.CompilerParams(vmem_limit_bytes=8 << 20)
    cost = pl.CostEstimate(flops=0, bytes_accessed=1 << 16, transcendentals=0)
    f32, bf16 = jnp.float32, jnp.bfloat16
    part = (quarter, width)
    raw = embeddings.reshape(blocks, rows, width)

    def pick(wanted, spread, held, after, name):
        n = len(wanted)
        shapes = [(len(numbers),) + part for numbers in wanted]
        if spread:
            shapes = shapes[:-n_x] + [(n_x,) + shapes[-1]]
        return pl.pallas_call(
            functools.partial(pick_kernel, wanted, spread),
            out_shape=[jax.ShapeDtypeStruct(shape, bf16) for shape in shapes],
            in_specs=[smem] + [hbm] * len(held + after),
            out_specs=[hbm] * len(shapes),
            scratch_shapes=[
                pltpu.VMEM((n, 4) + part, bf16),
                pltpu.SemaphoreType.DMA((4 * n,)),
                pltpu.SemaphoreType.DMA((n,)),
            ],
            compiler_params=middle,
            cost_estimate=cost,
            name=name,
        )(plan, *held, *after)

    def compare(stage, feeds, arrays, past, after, name):
        slots = len(stages[stage])
        shapes = [(2 * blocks, rows), (slots, quarter)]
        if past:
            shapes = [(2 * blocks, rows), (2 * chips, quarter), (blocks, rows)]
        return pl.pallas_call(
            functools.partial(pair_kernel, stage, feeds),
            out_shape=[jax.ShapeDtypeStruct(shape, f32) for shape in shapes],
            in_specs=[smem, pinned] + [vmem] * len(past) + [hbm] * len(arrays + after),
            out_specs=[vmem] * len(shapes),
            scratch_shapes=[
                pltpu.VMEM((2 * blocks, rows, width), bf16),
                pltpu.VMEM((slots,) + part, bf16),
                pltpu.VMEM((slots // 8 * 8 + 8, quarter), f32),
                pltpu.SemaphoreType.DMA((2 * blocks,)),
                pltpu.SemaphoreType.DMA((len(feeds),)),
            ],
            compiler_params=middle,
            cost_estimate=cost,
            name=name,
        )(plan, units, *past, *arrays, *after)

    def numbers(wanted):
        return [[every.index(slot) for slot in slots] for slots in wanted]

    cols, *away = pl.pallas_call(
        prep_kernel,
        out_shape=[jax.ShapeDtypeStruct((blocks,) + part, bf16)]
        + [jax.ShapeDtypeStruct((1,) + part, bf16)] * n_x,
        in_specs=[smem, hbm],
        out_specs=[hbm] * (1 + n_x),
        scratch_shapes=[
            pltpu.VMEM((blocks,) + part, bf16),
            pltpu.VMEM((blocks,) + part, bf16),
            pltpu.SemaphoreType.DMA((blocks,)),
            pltpu.SemaphoreType.DMA((n_x,)),
        ],
        compiler_params=params,
        cost_estimate=cost,
        name="prep",
    )(pair_table, raw)
    swap = [(0, 1), (1, 0)]
    sib_raw = lax.ppermute(raw, "core", swap)
    hop1 = move(cols, 0, 1)
    away = [move(a, dx, -2) for dx, a in enumerate(away)]
    plan = pl.pallas_call(
        plan_kernel,
        out_shape=jax.ShapeDtypeStruct((plan_size,), jnp.int32),
        in_specs=[smem, smem, hbm],
        out_specs=smem,
        scratch_shapes=[pltpu.SMEM((2 * blocks,), jnp.int32)],
        compiler_params=params,
        cost_estimate=cost,
        name="plan",
    )(pair_table, valid_rows, cols)
    units, local_best = pl.pallas_call(
        local_kernel,
        grid=(2 * blocks,),
        out_shape=(
            jax.ShapeDtypeStruct((2 * blocks, rows, width), bf16),
            jax.ShapeDtypeStruct((blocks, rows), f32),
        ),
        in_specs=[
            smem,
            pl.BlockSpec((1, rows, width), lambda i: (jnp.minimum(i, blocks - 1), 0, 0)),
            pl.BlockSpec((1, rows, width), lambda i: (jnp.maximum(i - blocks, 0), 0, 0)),
            pl.BlockSpec((blocks,) + part, lambda i: (0, 0, 0)),
        ],
        out_specs=(
            pl.BlockSpec((1, rows, width), lambda i: (i, 0, 0)),
            pl.BlockSpec((blocks, rows), lambda i: (0, 0)),
        ),
        compiler_params=params,
        cost_estimate=cost,
        name="local",
    )(valid_rows, raw, sib_raw, cols)
    hop1, away, local_best, plan = lax.optimization_barrier((hop1, away, local_best, plan))
    hop2 = move(hop1, 0, 1)
    away = move(jnp.concatenate(away, axis=0), 0, -2)
    wanted = [slots + down if slots[0][0] == 2 else slots for slots in first]
    picked = pick(numbers(wanted), False, [cols, hop1], [], "pick_a")
    first_in = [move(a, dx, 0) for dx, a in enumerate(picked)]
    hop2, away, *first_in = lax.optimization_barrier((hop2, away, *first_in))
    wanted = third + [extra]
    picked = pick(numbers(wanted + second), True, [cols, hop2], [], "pick_b")
    third_in = [move(a, slots[0][0], 1) for slots, a in zip(wanted, picked)]
    second_in = lax.all_to_all(picked[-1], "x", split_axis=0, concat_axis=0, tiled=True)
    down_in = move(first_in[2][3:], 0, -3)

    past_a = compare(
        0,
        [(dx, None, 3, 3 * dx) for dx in range(n_x)] + [(n_x, None, n_x, 3 * n_x)],
        first_in + [away],
        [],
        [picked[0]],
        "pairs_a",
    )
    past_b = compare(
        1,
        [(0, None, 2, 0), (1, None, 2, 2)],
        third_in[:2],
        [],
        [past_a[0]],
        "pairs_b",
    )
    row_best, col_best, sib_best = compare(
        2,
        [(0, None, 2, 0), (1, None, 1, 2), (2, None, 1, 3)]
        + [(3, dx, 2, 4 + 2 * dx) for dx in range(n_x)],
        [third_in[2], third_in[3], down_in, second_in],
        [*past_a, *past_b],
        [],
        "pairs_c",
    )
    sib_rows = lax.ppermute(sib_best, "core", swap)
    back = lax.all_to_all(col_best, ("x", "z"), split_axis=0, concat_axis=0, tiled=True)
    blended = pl.pallas_call(
        blend_kernel,
        out_shape=jax.ShapeDtypeStruct((blocks, rows), f32),
        in_specs=[vmem, vmem, vmem],
        out_specs=vmem,
        compiler_params=small,
        cost_estimate=cost,
        name="blend",
    )(local_best, row_best, sib_rows)
    combined = pl.pallas_call(
        merge_kernel,
        out_shape=jax.ShapeDtypeStruct((blocks, rows), f32),
        in_specs=[smem, vmem, vmem],
        out_specs=vmem,
        scratch_shapes=[pltpu.VMEM((blocks, quarter), f32)],
        compiler_params=small,
        cost_estimate=cost,
        name="merge",
    )(plan, blended, back)
    others = [
        lax.ppermute(combined, "rep", [(y, (y + d) % n_rep) for y in range(n_rep)])
        for d in range(1, n_rep)
    ]
    result = pl.pallas_call(
        finish_kernel,
        out_shape=jax.ShapeDtypeStruct((blocks * n_rep, quarter), f32),
        in_specs=[vmem, vmem, vmem, vmem],
        out_specs=vmem,
        compiler_params=small,
        cost_estimate=cost,
        name="finish",
    )(combined, *others)
    return result.reshape(-1)


def solution(mesh):
    grid = Mesh(mesh.devices.reshape(n_x, n_z, n_core, n_rep), ("x", "z", "core", "rep"))
    return jax.shard_map(
        on_device,
        mesh=grid,
        in_specs=(P(("x", "z", "core"), None), P(), P()),
        out_specs=P(("x", "z", "core")),
        check_vma=False,
    )
```

```python
import functools

import jax
import jax.numpy as jnp
from jax import lax
from jax.experimental import pallas as pl
from jax.experimental.pallas import tpu as pltpu
from jax.sharding import Mesh, PartitionSpec as P

absent = -2.0
epsilon = 1e-06
n_x, n_z, n_core, n_rep = 4, 8, 2, 4
chips = n_x * n_z
blocks = 8
rows = 512
quarter = rows // n_rep
width = 768
vmem_bytes = 60 << 20


def dot_t(left, right):
    return lax.dot_general(
        left, right, (((1,), (1,)), ((), ())), preferred_element_type=jnp.float32
    )


def normalise(raw):
    wide = raw.astype(jnp.float32)
    scale = lax.rsqrt(jnp.sum(wide * wide, axis=-1, keepdims=True) + epsilon)
    return (wide * scale).astype(jnp.bfloat16)


def place():
    return lax.axis_index("x"), lax.axis_index("z"), lax.axis_index("core"), lax.axis_index("rep")


def pair_info(table, source, target, core, many, which):
    side = which if many == 2 else jnp.where(source < target, core, 1 - core)
    forth = table[source * n_core + core, target * n_core + side]
    back = table[target * n_core + side, source * n_core + core]
    live = (forth >= 0) | (back >= 0)
    if many == 1:
        live = live & ((source != target) | (core == 0))
    source_block = jnp.where(forth >= 0, forth >> 3, back & 7)
    target_block = jnp.where(forth >= 0, forth & 7, (back >> 3) & 7)
    return live, side, source_block, target_block


def chip_at(x, z, dx, dz):
    return ((x + dx + n_x) & (n_x - 1)) * n_z + ((z + dz + n_z) & (n_z - 1))


first = [[(dx, 0, 1, 0), (dx, 1, 2, 0), (dx, 1, 2, 1)] for dx in range(n_x)]
second = [[(dx, 2, 2, 0), (dx, 2, 2, 1)] for dx in range(n_x)]
third = [[(dx, 3, 2, 0), (dx, 3, 2, 1)] for dx in (0, 1, 3)]
far = [(dx, 4, 1, 0) for dx in range(n_x)]
down = [(2, 5, 2, 0), (2, 5, 2, 1)]
stages = [sum(first, []) + far, down + third[0] + third[1], third[2] + sum(second, [])]
every = sum(stages, [])
gone_of = {0: 0, 1: 1, 2: 2, 3: 2}
at_pick, at_back, at_back_row, at_row, at_own = 0, 32, 64, 96, 128
at_stage, plan_size = [], 144
for stage in stages:
    at_stage.append(plan_size)
    plan_size += 16 + len(stage) + 1 + 1 + 3 * (len(stage) + 2)


def places(stage, base):
    slots = len(stage)
    counts = base + 2 * blocks
    groups = counts + slots + 1
    own_of = groups + 1
    return counts, groups, own_of, own_of + slots + 2, own_of + 2 * (slots + 2)


def plan_kernel(table, valid, after, plan, latest):
    x, z, core, rep = place()
    chip = chip_at(x, z, 0, 0)
    start = rep * quarter
    for o in range(2 * blocks):
        owner = chip * n_core + (core if o < blocks else 1 - core)
        plan[at_own + o] = valid[owner * blocks + o % blocks]
    number = 0
    for stage, base in zip(stages, at_stage):
        slots = len(stage)
        counts, groups, own_of, first_of, second_of = places(stage, base)
        for o in range(2 * blocks):
            plan[base + o] = 0
            latest[o] = 0
        plan[groups] = 0
        for slot, (dx, dz, many, which) in enumerate(stage):
            target = chip_at(x, z, dx, dz)
            _, _, block, _ = pair_info(table, chip, target, core, many, which)
            plan[at_back + number] = block
            plan[at_back_row + number] = 2 * target + which
            if dz in gone_of:
                gone = gone_of[dz]
                source, target = chip_at(x, z, 0, -gone), chip_at(x, z, dx, dz - gone)
                _, _, block, _ = pair_info(table, source, target, core, many, which)
                plan[at_pick + number] = block
            source = chip_at(x, z, -dx, -dz)
            live, side, block, own_block = pair_info(table, source, chip, core, many, which)
            mine = jnp.where(side == core, 0, blocks) + own_block
            count = plan[groups]
            joins = (plan[base + mine] & 1) == 1
            group = jnp.where(live, jnp.where(joins, latest[mine], count), slots + 1)
            plan[own_of + group] = mine
            plan[first_of + group] = jnp.where(joins, plan[first_of + group], slot)
            plan[second_of + group] = jnp.where(joins, slot, slots)
            latest[mine] = jnp.where(live, group, latest[mine])
            plan[groups] = count + (live & jnp.logical_not(joins)).astype(jnp.int32)
            plan[base + mine] = plan[base + mine] + live.astype(jnp.int32)
            plan[counts + slot] = valid[(source * n_core + core) * blocks + block] - start
            plan[at_row + number] = 2 * source + which
            number += 1
        plan[counts + slots] = 0
        count = plan[groups]
        plan[own_of + count] = plan[own_of]
        plan[first_of + count] = slots
        plan[second_of + count] = slots


def prep_kernel(table, emb, units, to0, to1, to2, to3, around, raw, unit, sem_in, sems):
    x, z, core, rep = place()
    chip = chip_at(x, z, 0, 0)
    loads = [
        pltpu.make_async_copy(emb.at[b, pl.ds(rep * quarter, quarter)], raw.at[b], sem_in.at[b])
        for b in range(blocks)
    ]
    for load in loads:
        load.start()
    copies = []
    for b in range(blocks):
        loads[b].wait()
        unit[b] = normalise(raw[b])
        copies.append(pltpu.make_async_copy(unit.at[b], units.at[b], sem_in.at[b]))
        copies[-1].start()
    outs = [to0.at[0], to1.at[0], to2.at[0], to3.at[0], around.at[0], around.at[1]]
    for a, (dx, dz, many, which) in enumerate(far + down):
        _, _, block, _ = pair_info(table, chip, chip_at(x, z, dx, dz), core, many, which)
        copies.append(pltpu.make_async_copy(unit.at[block], outs[a], sems.at[a]))
        copies[-1].start()
    for copy in copies:
        copy.wait()


def pick_kernel(wanted, spread, plan, *refs):
    near_by, hop = refs[:2]
    parts, get_sems, put_sems = refs[-3:]
    x, z, core, rep = place()
    n = len(wanted)
    if spread:
        outs = list(refs[-n + n_x - 4 : -4])
        outs += [refs[-4].at[(x + dx) & (n_x - 1)] for dx in range(n_x)]
    else:
        outs = refs[-n - 3 : -3]
    gets, puts = [], []
    for a, numbers in enumerate(wanted):
        for place_in, number in enumerate(numbers):
            held = near_by if every[number][1] == 0 else hop
            gets.append(
                pltpu.make_async_copy(
                    held.at[plan[at_pick + number]],
                    parts.at[a, place_in],
                    get_sems.at[3 * a + place_in],
                )
            )
            gets[-1].start()
    left = list(gets)
    for a, (out, numbers) in enumerate(zip(outs, wanted)):
        for _ in numbers:
            left.pop(0).wait()
        puts.append(
            pltpu.make_async_copy(parts.at[a, pl.ds(0, len(numbers))], out, put_sems.at[a])
        )
        puts[-1].start()
    for copy in puts:
        copy.wait()


def local_kernel(valid, own, sib, cols, unit_out, best):
    step = pl.program_id(0)
    x, z, core, rep = place()
    dev = chip_at(x, z, 0, 0) * n_core + core
    start = rep * quarter

    @pl.when(step >= blocks)
    def _():
        unit_out[0] = normalise(sib[0])

    @pl.when(step < blocks)
    def _():
        mine = normalise(own[0])
        unit_out[0] = mine
        part = lax.broadcasted_iota(jnp.int32, (quarter, rows), 0)
        gap = lax.broadcasted_iota(jnp.int32, (quarter, rows), 1) - part
        found = jnp.full((1, rows), absent, jnp.float32)
        for k in range(0, blocks, 2):
            pair = jnp.concatenate([cols[k], cols[k + 1]], axis=0)
            scores = dot_t(pair, mine)
            for half in range(2):
                count = valid[dev * blocks + k + half] - start
                own_gap = jnp.where(k + half == step, start, rows)
                allowed = (part < count) & (gap != own_gap)
                here = jnp.where(allowed, scores[half * quarter : (half + 1) * quarter], absent)
                found = jnp.maximum(found, jnp.max(here, axis=0, keepdims=True))
        best[pl.ds(step, 1), :] = found


def pair_kernel(stage, feeds, plan, own, *refs):
    final = stage == len(stages) - 1
    slots, base = len(stages[stage]), at_stage[stage]
    counts, groups, own_of, first_of, second_of = places(stages[stage], base)
    units, held, cols, sem_u, sem_g = refs[-5:]
    outs, arrays, past = refs[-8 if final else -7 : -5], refs, ()
    if final:
        past, arrays = refs[: 2 * stage], refs[2 * stage :]
    x, z, core, rep = place()
    gets = []
    for a, (array, dx, count, first_slot) in enumerate(feeds):
        came = arrays[array] if dx is None else arrays[array].at[(x - dx + n_x) & (n_x - 1)]
        gets.append(pltpu.make_async_copy(came, held.at[pl.ds(first_slot, count)], sem_g.at[a]))
        gets[-1].start()
    loads = []
    for o in range(2 * blocks):
        loads.append(pltpu.make_async_copy(own.at[o], units.at[o], sem_u.at[o]))

        @pl.when(plan[base + o] > 0)
        def _():
            loads[o].start()

    row_out, col_out = outs[:2]
    row_out[...] = jnp.full((2 * blocks, rows), absent, jnp.float32)
    for ref in past[::2]:
        row_out[...] = jnp.maximum(row_out[...], ref[...])
    cols[...] = jnp.full(cols.shape, absent, jnp.float32)
    if final:
        col_out[...] = jnp.full(col_out.shape, absent, jnp.float32)
        number = 0
        for ref, done in zip(past[1::2], stages):
            for slot in range(len(done)):
                col_out[pl.ds(plan[at_row + number], 1), :] = ref[slot : slot + 1, :]
                number += 1
    part = lax.broadcasted_iota(jnp.int32, (quarter, rows), 0)
    lane = lax.broadcasted_iota(jnp.int32, (2 * quarter, rows), 1)
    for copy in gets:
        copy.wait()
    for o in range(2 * blocks):

        @pl.when(plan[base + o] > 0)
        def _():
            loads[o].wait()

    def visit(turn, carry):
        for group in (2 * turn, 2 * turn + 1):
            o = plan[own_of + group]
            pair = [plan[first_of + group], plan[second_of + group]]
            here_slot = [jnp.minimum(slot, slots - 1) for slot in pair]
            scores = dot_t(
                jnp.concatenate([held[here_slot[0]], held[here_slot[1]]], axis=0), units[o]
            )
            ok = jnp.where(lane < plan[at_own + o], scores, absent)
            folded = jnp.maximum(
                jnp.maximum(ok[:, 0:128], ok[:, 128:256]), jnp.maximum(ok[:, 256:384], ok[:, 384:512])
            )
            top = jnp.full((1, rows), absent, jnp.float32)
            for half in range(2):
                span = slice(half * quarter, (half + 1) * quarter)
                here = jnp.where(part < plan[counts + pair[half]], scores[span], absent)
                top = jnp.maximum(top, jnp.max(here, axis=0, keepdims=True))
                cols[pl.ds(pair[half], 1), :] = jnp.max(folded[span].T, axis=0, keepdims=True)
            row_out[pl.ds(o, 1), :] = jnp.maximum(row_out[pl.ds(o, 1), :], top)
        return carry

    lax.fori_loop(0, (plan[groups] + 1) >> 1, visit, 0)
    if final:
        outs[2][...] = row_out[blocks:]
        for slot in range(slots):
            number = len(every) - slots + slot
            col_out[pl.ds(plan[at_row + number], 1), :] = cols[slot : slot + 1, :]
    else:
        col_out[...] = cols[0:slots]


def spread_in(running, best, rep):
    wide = jnp.concatenate([best] * n_rep, axis=1)
    lane = lax.broadcasted_iota(jnp.int32, (blocks, rows), 1)
    mine = (lane >= rep * quarter) & (lane < (rep + 1) * quarter)
    return jnp.where(mine, jnp.maximum(running, wide), running)


def blend_kernel(local, row_best, sib_rows, out):
    out[...] = jnp.maximum(jnp.maximum(local[...], row_best[0:blocks]), sib_rows[...])


def merge_kernel(plan, blended, back, out, best):
    rep = lax.axis_index("rep")
    best[...] = jnp.full((blocks, quarter), absent, jnp.float32)
    for number in range(len(every)):
        block = plan[at_back + number]
        best[pl.ds(block, 1), :] = jnp.maximum(
            best[pl.ds(block, 1), :], back[pl.ds(plan[at_back_row + number], 1), :]
        )
    merged = spread_in(blended[...], best[...], rep)
    lane = lax.broadcasted_iota(jnp.int32, (1, rows), 1)
    for b in range(blocks):
        out[b : b + 1, :] = jnp.where(lane < plan[at_own + b], merged[b : b + 1], -1.0)


def finish_kernel(one, two, three, four, out):
    best = jnp.maximum(jnp.maximum(one[...], two[...]), jnp.maximum(three[...], four[...]))
    for b in range(blocks):
        for q in range(n_rep):
            out[n_rep * b + q : n_rep * b + q + 1, :] = best[
                b : b + 1, q * quarter : (q + 1) * quarter
            ]


def move(value, dx, dz):
    if dx % n_x == 0 and dz % n_z == 0:
        return value
    steps = [
        (x * n_z + z, (x + dx) % n_x * n_z + (z + dz) % n_z) for x in range(n_x) for z in range(n_z)
    ]
    return lax.ppermute(value, ("x", "z"), steps)


def on_device(embeddings, valid_rows, pair_table):
    smem = pl.BlockSpec(memory_space=pltpu.SMEM)
    vmem = pl.BlockSpec(memory_space=pltpu.VMEM)
    hbm = pl.BlockSpec(memory_space=pl.ANY)
    pinned = pl.BlockSpec(memory_space=pltpu.HBM)
    params = pltpu.CompilerParams(vmem_limit_bytes=vmem_bytes)
    middle = pltpu.CompilerParams(vmem_limit_bytes=56 << 20)
    small = pltpu.CompilerParams(vmem_limit_bytes=8 << 20)
    cost = pl.CostEstimate(flops=0, bytes_accessed=1 << 16, transcendentals=0)
    f32, bf16 = jnp.float32, jnp.bfloat16
    part = (quarter, width)
    raw = embeddings.reshape(blocks, rows, width)

    def pick(wanted, spread, held, after, name):
        n = len(wanted)
        shapes = [(len(numbers),) + part for numbers in wanted]
        if spread:
            shapes = shapes[:-n_x] + [(n_x,) + shapes[-1]]
        return pl.pallas_call(
            functools.partial(pick_kernel, wanted, spread),
            out_shape=[jax.ShapeDtypeStruct(shape, bf16) for shape in shapes],
            in_specs=[smem] + [hbm] * len(held + after),
            out_specs=[hbm] * len(shapes),
            scratch_shapes=[
                pltpu.VMEM((n, 3) + part, bf16),
                pltpu.SemaphoreType.DMA((3 * n,)),
                pltpu.SemaphoreType.DMA((n,)),
            ],
            compiler_params=middle,
            cost_estimate=cost,
            name=name,
        )(plan, *held, *after)

    def compare(stage, feeds, arrays, past, after, name):
        slots = len(stages[stage])
        shapes = [(2 * blocks, rows), (slots, quarter)]
        if past:
            shapes = [(2 * blocks, rows), (2 * chips, quarter), (blocks, rows)]
        return pl.pallas_call(
            functools.partial(pair_kernel, stage, feeds),
            out_shape=[jax.ShapeDtypeStruct(shape, f32) for shape in shapes],
            in_specs=[smem, pinned] + [vmem] * len(past) + [hbm] * len(arrays + after),
            out_specs=[vmem] * len(shapes),
            scratch_shapes=[
                pltpu.VMEM((2 * blocks, rows, width), bf16),
                pltpu.VMEM((slots,) + part, bf16),
                pltpu.VMEM((slots // 8 * 8 + 8, quarter), f32),
                pltpu.SemaphoreType.DMA((2 * blocks,)),
                pltpu.SemaphoreType.DMA((len(feeds),)),
            ],
            compiler_params=middle,
            cost_estimate=cost,
            name=name,
        )(plan, units, *past, *arrays, *after)

    def numbers(wanted):
        return [[every.index(slot) for slot in slots] for slots in wanted]

    cols, *away, around = pl.pallas_call(
        prep_kernel,
        out_shape=[jax.ShapeDtypeStruct((blocks,) + part, bf16)]
        + [jax.ShapeDtypeStruct((1,) + part, bf16)] * n_x
        + [jax.ShapeDtypeStruct((2,) + part, bf16)],
        in_specs=[smem, hbm],
        out_specs=[hbm] * (2 + n_x),
        scratch_shapes=[
            pltpu.VMEM((blocks,) + part, bf16),
            pltpu.VMEM((blocks,) + part, bf16),
            pltpu.SemaphoreType.DMA((blocks,)),
            pltpu.SemaphoreType.DMA((len(far + down),)),
        ],
        compiler_params=params,
        cost_estimate=cost,
        name="prep",
    )(pair_table, raw)
    swap = [(0, 1), (1, 0)]
    sib_raw = lax.ppermute(raw, "core", swap)
    hop1 = move(cols, 0, 1)
    away = [move(a, dx, -2) for dx, a in enumerate(away)]
    plan = pl.pallas_call(
        plan_kernel,
        out_shape=jax.ShapeDtypeStruct((plan_size,), jnp.int32),
        in_specs=[smem, smem, hbm],
        out_specs=smem,
        scratch_shapes=[pltpu.SMEM((2 * blocks,), jnp.int32)],
        compiler_params=params,
        cost_estimate=cost,
        name="plan",
    )(pair_table, valid_rows, cols)
    units, local_best = pl.pallas_call(
        local_kernel,
        grid=(2 * blocks,),
        out_shape=(
            jax.ShapeDtypeStruct((2 * blocks, rows, width), bf16),
            jax.ShapeDtypeStruct((blocks, rows), f32),
        ),
        in_specs=[
            smem,
            pl.BlockSpec((1, rows, width), lambda i: (jnp.minimum(i, blocks - 1), 0, 0)),
            pl.BlockSpec((1, rows, width), lambda i: (jnp.maximum(i - blocks, 0), 0, 0)),
            pl.BlockSpec((blocks,) + part, lambda i: (0, 0, 0)),
        ],
        out_specs=(
            pl.BlockSpec((1, rows, width), lambda i: (i, 0, 0)),
            pl.BlockSpec((blocks, rows), lambda i: (0, 0)),
        ),
        compiler_params=params,
        cost_estimate=cost,
        name="local",
    )(valid_rows, raw, sib_raw, cols)
    hop1, away, local_best, plan = lax.optimization_barrier((hop1, away, local_best, plan))
    hop2 = move(hop1, 0, 1)
    away = move(jnp.concatenate(away, axis=0), 0, -2)
    picked = pick(numbers(first), False, [cols, hop1], [], "pick_a")
    first_in = [move(a, dx, 0) for dx, a in enumerate(picked)]
    hop2, away, around, *first_in = lax.optimization_barrier((hop2, away, around, *first_in))
    down_in = move(around, 2, -3)
    picked = pick(numbers(third + second), True, [cols, hop2], [], "pick_b")
    third_in = [move(a, slots[0][0], 1) for slots, a in zip(third, picked)]
    second_in = lax.all_to_all(picked[-1], "x", split_axis=0, concat_axis=0, tiled=True)

    past_a = compare(
        0,
        [(dx, None, 3, 3 * dx) for dx in range(n_x)] + [(n_x, None, n_x, 3 * n_x)],
        first_in + [away],
        [],
        [picked[0]],
        "pairs_a",
    )
    past_b = compare(
        1,
        [(0, None, 2, 0), (1, None, 2, 2), (2, None, 2, 4)],
        [down_in] + third_in[:2],
        [],
        [past_a[0]],
        "pairs_b",
    )
    row_best, col_best, sib_best = compare(
        2,
        [(0, None, 2, 0)] + [(1, dx, 2, 2 + 2 * dx) for dx in range(n_x)],
        [third_in[2], second_in],
        [*past_a, *past_b],
        [],
        "pairs_c",
    )
    sib_rows = lax.ppermute(sib_best, "core", swap)
    back = lax.all_to_all(col_best, ("x", "z"), split_axis=0, concat_axis=0, tiled=True)
    blended = pl.pallas_call(
        blend_kernel,
        out_shape=jax.ShapeDtypeStruct((blocks, rows), f32),
        in_specs=[vmem, vmem, vmem],
        out_specs=vmem,
        compiler_params=small,
        cost_estimate=cost,
        name="blend",
    )(local_best, row_best, sib_rows)
    combined = pl.pallas_call(
        merge_kernel,
        out_shape=jax.ShapeDtypeStruct((blocks, rows), f32),
        in_specs=[smem, vmem, vmem],
        out_specs=vmem,
        scratch_shapes=[pltpu.VMEM((blocks, quarter), f32)],
        compiler_params=small,
        cost_estimate=cost,
        name="merge",
    )(plan, blended, back)
    others = [
        lax.ppermute(combined, "rep", [(y, (y + d) % n_rep) for y in range(n_rep)])
        for d in range(1, n_rep)
    ]
    result = pl.pallas_call(
        finish_kernel,
        out_shape=jax.ShapeDtypeStruct((blocks * n_rep, quarter), f32),
        in_specs=[vmem, vmem, vmem, vmem],
        out_specs=vmem,
        compiler_params=small,
        cost_estimate=cost,
        name="finish",
    )(combined, *others)
    return result.reshape(-1)


def solution(mesh):
    grid = Mesh(mesh.devices.reshape(n_x, n_z, n_core, n_rep), ("x", "z", "core", "rep"))
    return jax.shard_map(
        on_device,
        mesh=grid,
        in_specs=(P(("x", "z", "core"), None), P(), P()),
        out_specs=P(("x", "z", "core")),
        check_vma=False,
    )
```

```python
import functools

import jax
import jax.numpy as jnp
from jax import lax
from jax.experimental import pallas as pl
from jax.experimental.pallas import tpu as pltpu
from jax.sharding import Mesh, PartitionSpec as P

absent = -2.0
epsilon = 1e-06
n_x, n_z, n_core, n_rep = 4, 8, 2, 4
chips = n_x * n_z
blocks = 8
rows = 512
quarter = rows // n_rep
width = 768
vmem_bytes = 60 << 20


def dot_t(left, right):
    return lax.dot_general(
        left, right, (((1,), (1,)), ((), ())), preferred_element_type=jnp.float32
    )


def normalise(raw):
    wide = raw.astype(jnp.float32)
    scale = lax.rsqrt(jnp.sum(wide * wide, axis=-1, keepdims=True) + epsilon)
    return (wide * scale).astype(jnp.bfloat16)


def place():
    return lax.axis_index("x"), lax.axis_index("z"), lax.axis_index("core"), lax.axis_index("rep")


def pair_info(table, source, target, core, many, which):
    side = which if many == 2 else jnp.where(source < target, core, 1 - core)
    forth = table[source * n_core + core, target * n_core + side]
    back = table[target * n_core + side, source * n_core + core]
    live = (forth >= 0) | (back >= 0)
    if many == 1:
        live = live & ((source != target) | (core == 0))
    source_block = jnp.where(forth >= 0, forth >> 3, back & 7)
    target_block = jnp.where(forth >= 0, forth & 7, (back >> 3) & 7)
    return live, side, source_block, target_block


def chip_at(x, z, dx, dz):
    return ((x + dx + n_x) & (n_x - 1)) * n_z + ((z + dz + n_z) & (n_z - 1))


first = [[(dx, 0, 1, 0), (dx, 1, 2, 0), (dx, 1, 2, 1)] for dx in range(n_x)]
second = [[(dx, 2, 2, 0), (dx, 2, 2, 1)] for dx in range(n_x)]
third = [[(dx, 3, 2, 0), (dx, 3, 2, 1)] for dx in (0, 1, 3)]
far = [(dx, 4, 1, 0) for dx in range(n_x)]
down = [(2, 5, 2, 0), (2, 5, 2, 1)]
stages = [sum(first, []) + far, third[0] + third[1], third[2] + down + sum(second, [])]
every = sum(stages, [])
gone_of = {0: 0, 1: 1, 2: 2, 3: 2}
at_pick, at_back, at_back_row, at_row, at_own = 0, 32, 64, 96, 128
at_stage, plan_size = [], 144
for stage in stages:
    at_stage.append(plan_size)
    plan_size += 16 + len(stage) + 1 + 1 + 3 * (len(stage) + 2)


def places(stage, base):
    slots = len(stage)
    counts = base + 2 * blocks
    groups = counts + slots + 1
    own_of = groups + 1
    return counts, groups, own_of, own_of + slots + 2, own_of + 2 * (slots + 2)


def plan_kernel(table, valid, after, plan, latest):
    x, z, core, rep = place()
    chip = chip_at(x, z, 0, 0)
    start = rep * quarter
    for o in range(2 * blocks):
        owner = chip * n_core + (core if o < blocks else 1 - core)
        plan[at_own + o] = valid[owner * blocks + o % blocks]
    number = 0
    for stage, base in zip(stages, at_stage):
        slots = len(stage)
        counts, groups, own_of, first_of, second_of = places(stage, base)
        for o in range(2 * blocks):
            plan[base + o] = 0
            latest[o] = 0
        plan[groups] = 0
        for slot, (dx, dz, many, which) in enumerate(stage):
            target = chip_at(x, z, dx, dz)
            _, _, block, _ = pair_info(table, chip, target, core, many, which)
            plan[at_back + number] = block
            plan[at_back_row + number] = 2 * target + which
            if dz in gone_of:
                gone = gone_of[dz]
                source, target = chip_at(x, z, 0, -gone), chip_at(x, z, dx, dz - gone)
                _, _, block, _ = pair_info(table, source, target, core, many, which)
                plan[at_pick + number] = block
            source = chip_at(x, z, -dx, -dz)
            live, side, block, own_block = pair_info(table, source, chip, core, many, which)
            mine = jnp.where(side == core, 0, blocks) + own_block
            count = plan[groups]
            joins = (plan[base + mine] & 1) == 1
            group = jnp.where(live, jnp.where(joins, latest[mine], count), slots + 1)
            plan[own_of + group] = mine
            plan[first_of + group] = jnp.where(joins, plan[first_of + group], slot)
            plan[second_of + group] = jnp.where(joins, slot, slots)
            latest[mine] = jnp.where(live, group, latest[mine])
            plan[groups] = count + (live & jnp.logical_not(joins)).astype(jnp.int32)
            plan[base + mine] = plan[base + mine] + live.astype(jnp.int32)
            plan[counts + slot] = valid[(source * n_core + core) * blocks + block] - start
            plan[at_row + number] = 2 * source + which
            number += 1
        plan[counts + slots] = 0
        count = plan[groups]
        plan[own_of + count] = plan[own_of]
        plan[first_of + count] = slots
        plan[second_of + count] = slots


def prep_kernel(table, emb, units, to0, to1, to2, to3, around, raw, unit, sem_in, sems):
    x, z, core, rep = place()
    chip = chip_at(x, z, 0, 0)
    loads = [
        pltpu.make_async_copy(emb.at[b, pl.ds(rep * quarter, quarter)], raw.at[b], sem_in.at[b])
        for b in range(blocks)
    ]
    for load in loads:
        load.start()
    copies = []
    for b in range(blocks):
        loads[b].wait()
        unit[b] = normalise(raw[b])
        copies.append(pltpu.make_async_copy(unit.at[b], units.at[b], sem_in.at[b]))
        copies[-1].start()
    outs = [to0.at[0], to1.at[0], to2.at[0], to3.at[0], around.at[0], around.at[1]]
    for a, (dx, dz, many, which) in enumerate(far + down):
        _, _, block, _ = pair_info(table, chip, chip_at(x, z, dx, dz), core, many, which)
        copies.append(pltpu.make_async_copy(unit.at[block], outs[a], sems.at[a]))
        copies[-1].start()
    for copy in copies:
        copy.wait()


def pick_kernel(wanted, spread, plan, *refs):
    near_by, hop = refs[:2]
    parts, get_sems, put_sems = refs[-3:]
    x, z, core, rep = place()
    n = len(wanted)
    if spread:
        outs = list(refs[-n + n_x - 4 : -4])
        outs += [refs[-4].at[(x + dx) & (n_x - 1)] for dx in range(n_x)]
    else:
        outs = refs[-n - 3 : -3]
    gets, puts = [], []
    for a, numbers in enumerate(wanted):
        for place_in, number in enumerate(numbers):
            held = near_by if every[number][1] == 0 else hop
            gets.append(
                pltpu.make_async_copy(
                    held.at[plan[at_pick + number]],
                    parts.at[a, place_in],
                    get_sems.at[3 * a + place_in],
                )
            )
            gets[-1].start()
    left = list(gets)
    for a, (out, numbers) in enumerate(zip(outs, wanted)):
        for _ in numbers:
            left.pop(0).wait()
        puts.append(
            pltpu.make_async_copy(parts.at[a, pl.ds(0, len(numbers))], out, put_sems.at[a])
        )
        puts[-1].start()
    for copy in puts:
        copy.wait()


def local_kernel(valid, own, sib, cols, unit_out, best):
    step = pl.program_id(0)
    x, z, core, rep = place()
    dev = chip_at(x, z, 0, 0) * n_core + core
    start = rep * quarter

    @pl.when(step >= blocks)
    def _():
        unit_out[0] = normalise(sib[0])

    @pl.when(step < blocks)
    def _():
        mine = normalise(own[0])
        unit_out[0] = mine
        part = lax.broadcasted_iota(jnp.int32, (quarter, rows), 0)
        gap = lax.broadcasted_iota(jnp.int32, (quarter, rows), 1) - part
        found = jnp.full((1, rows), absent, jnp.float32)
        for k in range(0, blocks, 2):
            pair = jnp.concatenate([cols[k], cols[k + 1]], axis=0)
            scores = dot_t(pair, mine)
            for half in range(2):
                count = valid[dev * blocks + k + half] - start
                own_gap = jnp.where(k + half == step, start, rows)
                allowed = (part < count) & (gap != own_gap)
                here = jnp.where(allowed, scores[half * quarter : (half + 1) * quarter], absent)
                found = jnp.maximum(found, jnp.max(here, axis=0, keepdims=True))
        best[pl.ds(step, 1), :] = found


def pair_kernel(stage, feeds, plan, own, *refs):
    final = stage == len(stages) - 1
    slots, base = len(stages[stage]), at_stage[stage]
    counts, groups, own_of, first_of, second_of = places(stages[stage], base)
    units, held, cols, sem_u, sem_g = refs[-5:]
    outs, arrays, past = refs[-8 if final else -7 : -5], refs, ()
    if final:
        past, arrays = refs[: 2 * stage], refs[2 * stage :]
    x, z, core, rep = place()
    gets = []
    for a, (array, dx, count, first_slot) in enumerate(feeds):
        came = arrays[array] if dx is None else arrays[array].at[(x - dx + n_x) & (n_x - 1)]
        gets.append(pltpu.make_async_copy(came, held.at[pl.ds(first_slot, count)], sem_g.at[a]))
        gets[-1].start()
    loads = []
    for o in range(2 * blocks):
        loads.append(pltpu.make_async_copy(own.at[o], units.at[o], sem_u.at[o]))

        @pl.when(plan[base + o] > 0)
        def _():
            loads[o].start()

    row_out, col_out = outs[:2]
    row_out[...] = jnp.full((2 * blocks, rows), absent, jnp.float32)
    for ref in past[::2]:
        row_out[...] = jnp.maximum(row_out[...], ref[...])
    cols[...] = jnp.full(cols.shape, absent, jnp.float32)
    if final:
        col_out[...] = jnp.full(col_out.shape, absent, jnp.float32)
        number = 0
        for ref, done in zip(past[1::2], stages):
            for slot in range(len(done)):
                col_out[pl.ds(plan[at_row + number], 1), :] = ref[slot : slot + 1, :]
                number += 1
    row = lax.broadcasted_iota(jnp.int32, (rows, quarter), 0)
    lane = lax.broadcasted_iota(jnp.int32, (rows, quarter), 1)
    for copy in gets:
        copy.wait()
    for o in range(2 * blocks):

        @pl.when(plan[base + o] > 0)
        def _():
            loads[o].wait()

    def visit(turn, carry):
        for group in (2 * turn, 2 * turn + 1):
            o = plan[own_of + group]
            pair = [plan[first_of + group], plan[second_of + group]]
            here_slot = [jnp.minimum(slot, slots - 1) for slot in pair]
            scores = dot_t(
                units[o], jnp.concatenate([held[here_slot[0]], held[here_slot[1]]], axis=0)
            )
            folded = jnp.full((rows, quarter), absent, jnp.float32)
            for half in range(2):
                here = scores[:, half * quarter : (half + 1) * quarter]
                ok = jnp.where(row < plan[at_own + o], here, absent)
                cols[pl.ds(pair[half], 1), :] = jnp.max(ok, axis=0, keepdims=True)
                ok = jnp.where(lane < plan[counts + pair[half]], here, absent)
                folded = jnp.maximum(folded, ok)
            top = jnp.concatenate(
                [
                    jnp.max(folded[k : k + quarter].T, axis=0, keepdims=True)
                    for k in range(0, rows, quarter)
                ],
                axis=1,
            )
            row_out[pl.ds(o, 1), :] = jnp.maximum(row_out[pl.ds(o, 1), :], top)
        return carry

    lax.fori_loop(0, (plan[groups] + 1) >> 1, visit, 0)
    if final:
        outs[2][...] = row_out[blocks:]
        for slot in range(slots):
            number = len(every) - slots + slot
            col_out[pl.ds(plan[at_row + number], 1), :] = cols[slot : slot + 1, :]
    else:
        col_out[...] = cols[0:slots]


def spread_in(running, best, rep):
    wide = jnp.concatenate([best] * n_rep, axis=1)
    lane = lax.broadcasted_iota(jnp.int32, (blocks, rows), 1)
    mine = (lane >= rep * quarter) & (lane < (rep + 1) * quarter)
    return jnp.where(mine, jnp.maximum(running, wide), running)


def blend_kernel(local, row_best, sib_rows, out):
    out[...] = jnp.maximum(jnp.maximum(local[...], row_best[0:blocks]), sib_rows[...])


def merge_kernel(plan, blended, back, out, best):
    rep = lax.axis_index("rep")
    best[...] = jnp.full((blocks, quarter), absent, jnp.float32)
    for number in range(len(every)):
        block = plan[at_back + number]
        best[pl.ds(block, 1), :] = jnp.maximum(
            best[pl.ds(block, 1), :], back[pl.ds(plan[at_back_row + number], 1), :]
        )
    merged = spread_in(blended[...], best[...], rep)
    lane = lax.broadcasted_iota(jnp.int32, (1, rows), 1)
    for b in range(blocks):
        out[b : b + 1, :] = jnp.where(lane < plan[at_own + b], merged[b : b + 1], -1.0)


def finish_kernel(one, two, three, four, out):
    best = jnp.maximum(jnp.maximum(one[...], two[...]), jnp.maximum(three[...], four[...]))
    for b in range(blocks):
        for q in range(n_rep):
            out[n_rep * b + q : n_rep * b + q + 1, :] = best[
                b : b + 1, q * quarter : (q + 1) * quarter
            ]


def move(value, dx, dz):
    if dx % n_x == 0 and dz % n_z == 0:
        return value
    steps = [
        (x * n_z + z, (x + dx) % n_x * n_z + (z + dz) % n_z) for x in range(n_x) for z in range(n_z)
    ]
    return lax.ppermute(value, ("x", "z"), steps)


def on_device(embeddings, valid_rows, pair_table):
    smem = pl.BlockSpec(memory_space=pltpu.SMEM)
    vmem = pl.BlockSpec(memory_space=pltpu.VMEM)
    hbm = pl.BlockSpec(memory_space=pl.ANY)
    pinned = pl.BlockSpec(memory_space=pltpu.HBM)
    params = pltpu.CompilerParams(vmem_limit_bytes=vmem_bytes)
    middle = pltpu.CompilerParams(vmem_limit_bytes=56 << 20)
    small = pltpu.CompilerParams(vmem_limit_bytes=8 << 20)
    cost = pl.CostEstimate(flops=0, bytes_accessed=1 << 16, transcendentals=0)
    f32, bf16 = jnp.float32, jnp.bfloat16
    part = (quarter, width)
    raw = embeddings.reshape(blocks, rows, width)

    def pick(wanted, spread, held, after, name):
        n = len(wanted)
        shapes = [(len(numbers),) + part for numbers in wanted]
        if spread:
            shapes = shapes[:-n_x] + [(n_x,) + shapes[-1]]
        return pl.pallas_call(
            functools.partial(pick_kernel, wanted, spread),
            out_shape=[jax.ShapeDtypeStruct(shape, bf16) for shape in shapes],
            in_specs=[smem] + [hbm] * len(held + after),
            out_specs=[hbm] * len(shapes),
            scratch_shapes=[
                pltpu.VMEM((n, 3) + part, bf16),
                pltpu.SemaphoreType.DMA((3 * n,)),
                pltpu.SemaphoreType.DMA((n,)),
            ],
            compiler_params=middle,
            cost_estimate=cost,
            name=name,
        )(plan, *held, *after)

    def compare(stage, feeds, arrays, past, after, name):
        slots = len(stages[stage])
        shapes = [(2 * blocks, rows), (slots, quarter)]
        if past:
            shapes = [(2 * blocks, rows), (2 * chips, quarter), (blocks, rows)]
        return pl.pallas_call(
            functools.partial(pair_kernel, stage, feeds),
            out_shape=[jax.ShapeDtypeStruct(shape, f32) for shape in shapes],
            in_specs=[smem, pinned] + [vmem] * len(past) + [hbm] * len(arrays + after),
            out_specs=[vmem] * len(shapes),
            scratch_shapes=[
                pltpu.VMEM((2 * blocks, rows, width), bf16),
                pltpu.VMEM((slots,) + part, bf16),
                pltpu.VMEM((slots // 8 * 8 + 8, quarter), f32),
                pltpu.SemaphoreType.DMA((2 * blocks,)),
                pltpu.SemaphoreType.DMA((len(feeds),)),
            ],
            compiler_params=middle,
            cost_estimate=cost,
            name=name,
        )(plan, units, *past, *arrays, *after)

    def numbers(wanted):
        return [[every.index(slot) for slot in slots] for slots in wanted]

    cols, *away, around = pl.pallas_call(
        prep_kernel,
        out_shape=[jax.ShapeDtypeStruct((blocks,) + part, bf16)]
        + [jax.ShapeDtypeStruct((1,) + part, bf16)] * n_x
        + [jax.ShapeDtypeStruct((2,) + part, bf16)],
        in_specs=[smem, hbm],
        out_specs=[hbm] * (2 + n_x),
        scratch_shapes=[
            pltpu.VMEM((blocks,) + part, bf16),
            pltpu.VMEM((blocks,) + part, bf16),
            pltpu.SemaphoreType.DMA((blocks,)),
            pltpu.SemaphoreType.DMA((len(far + down),)),
        ],
        compiler_params=params,
        cost_estimate=cost,
        name="prep",
    )(pair_table, raw)
    swap = [(0, 1), (1, 0)]
    sib_raw = lax.ppermute(raw, "core", swap)
    hop1 = move(cols, 0, 1)
    away = [move(a, dx, -2) for dx, a in enumerate(away)]
    plan = pl.pallas_call(
        plan_kernel,
        out_shape=jax.ShapeDtypeStruct((plan_size,), jnp.int32),
        in_specs=[smem, smem, hbm],
        out_specs=smem,
        scratch_shapes=[pltpu.SMEM((2 * blocks,), jnp.int32)],
        compiler_params=params,
        cost_estimate=cost,
        name="plan",
    )(pair_table, valid_rows, cols)
    units, local_best = pl.pallas_call(
        local_kernel,
        grid=(2 * blocks,),
        out_shape=(
            jax.ShapeDtypeStruct((2 * blocks, rows, width), bf16),
            jax.ShapeDtypeStruct((blocks, rows), f32),
        ),
        in_specs=[
            smem,
            pl.BlockSpec((1, rows, width), lambda i: (jnp.minimum(i, blocks - 1), 0, 0)),
            pl.BlockSpec((1, rows, width), lambda i: (jnp.maximum(i - blocks, 0), 0, 0)),
            pl.BlockSpec((blocks,) + part, lambda i: (0, 0, 0)),
        ],
        out_specs=(
            pl.BlockSpec((1, rows, width), lambda i: (i, 0, 0)),
            pl.BlockSpec((blocks, rows), lambda i: (0, 0)),
        ),
        compiler_params=params,
        cost_estimate=cost,
        name="local",
    )(valid_rows, raw, sib_raw, cols)
    hop1, away, local_best, plan = lax.optimization_barrier((hop1, away, local_best, plan))
    hop2 = move(hop1, 0, 1)
    away = move(jnp.concatenate(away, axis=0), 0, -2)
    picked = pick(numbers(first), False, [cols, hop1], [], "pick_a")
    first_in = [move(a, dx, 0) for dx, a in enumerate(picked)]
    hop2, away, around, *first_in = lax.optimization_barrier((hop2, away, around, *first_in))
    picked = pick(numbers(third + second), True, [cols, hop2], [], "pick_b")
    third_in = [move(a, slots[0][0], 1) for slots, a in zip(third, picked)]
    second_in = lax.all_to_all(picked[-1], "x", split_axis=0, concat_axis=0, tiled=True)
    down_in = move(around, 2, -3)

    past_a = compare(
        0,
        [(dx, None, 3, 3 * dx) for dx in range(n_x)] + [(n_x, None, n_x, 3 * n_x)],
        first_in + [away],
        [],
        [picked[0]],
        "pairs_a",
    )
    past_b = compare(
        1,
        [(0, None, 2, 0), (1, None, 2, 2)],
        third_in[:2],
        [],
        [past_a[0]],
        "pairs_b",
    )
    row_best, col_best, sib_best = compare(
        2,
        [(0, None, 2, 0), (1, None, 2, 2)] + [(2, dx, 2, 4 + 2 * dx) for dx in range(n_x)],
        [third_in[2], down_in, second_in],
        [*past_a, *past_b],
        [],
        "pairs_c",
    )
    sib_rows = lax.ppermute(sib_best, "core", swap)
    back = lax.all_to_all(col_best, ("x", "z"), split_axis=0, concat_axis=0, tiled=True)
    blended = pl.pallas_call(
        blend_kernel,
        out_shape=jax.ShapeDtypeStruct((blocks, rows), f32),
        in_specs=[vmem, vmem, vmem],
        out_specs=vmem,
        compiler_params=small,
        cost_estimate=cost,
        name="blend",
    )(local_best, row_best, sib_rows)
    combined = pl.pallas_call(
        merge_kernel,
        out_shape=jax.ShapeDtypeStruct((blocks, rows), f32),
        in_specs=[smem, vmem, vmem],
        out_specs=vmem,
        scratch_shapes=[pltpu.VMEM((blocks, quarter), f32)],
        compiler_params=small,
        cost_estimate=cost,
        name="merge",
    )(plan, blended, back)
    others = [
        lax.ppermute(combined, "rep", [(y, (y + d) % n_rep) for y in range(n_rep)])
        for d in range(1, n_rep)
    ]
    result = pl.pallas_call(
        finish_kernel,
        out_shape=jax.ShapeDtypeStruct((blocks * n_rep, quarter), f32),
        in_specs=[vmem, vmem, vmem, vmem],
        out_specs=vmem,
        compiler_params=small,
        cost_estimate=cost,
        name="finish",
    )(combined, *others)
    return result.reshape(-1)


def solution(mesh):
    grid = Mesh(mesh.devices.reshape(n_x, n_z, n_core, n_rep), ("x", "z", "core", "rep"))
    return jax.shard_map(
        on_device,
        mesh=grid,
        in_specs=(P(("x", "z", "core"), None), P(), P()),
        out_specs=P(("x", "z", "core")),
        check_vma=False,
    )
```
